32 devices in a mesh: grp: 4 (over y, x), row: 8 (over z, core).
Axes of the slice: x: 2, y: 2, z: 4, core: 2. Of those that a mesh axis runs over, the one named last changes fastest.
Arguments:
- colatitude: float32 [65536], P(('grp', 'row')), may hold values from 0.05 to 3.09
- longitude: float32 [65536], P(('grp', 'row')), may hold values from -3.140625 to 3.140625
- observed: bfloat16 [2, 65536], P(None, ('grp', 'row')), may hold values from -6 to 6
- filter_taps: bfloat16 [2, 256], replicated, may hold values from -0.375 to 0.375
- segment_start: int32 [65536], P(('grp', 'row')), may hold values 0 or 1
- harmonic: int32 [2, 512], replicated, may hold values from -280 to 280, as said below
Outputs:
- normal: float32 [512, 512], P('row', 'grp')
- right_side: float32 [512], replicated
- diagonal: float32 [512], replicated
The draws below stay inside these ranges and needn't reach their ends.
Inputs may be any that keep to these rules, and one draw needn't show every extreme that they name: `harmonic`: row 0 holds degrees from 2 to 280; row 1 holds orders whose magnitude is at most the column's degree; no two columns name the same pair; the pairs (280, 280) and (280, -280) are always present.
All inputs are finite; a program needn't handle non-finite values. No bound on the sum of `segment_start` on one device may be relied on, other than what follows from the above.
Results may differ from the reference program's by a relative error of at most 0.0041.
Values may be sent and summed in bfloat16 or wider, within the bound.
A program may use at most 64 MiB of HBM per device.

```python
import jax
import jax.numpy as jnp
from jax import lax

PANEL = 512
TAPS = 256
NMAX = 280
ROWS_DEV = 2048
ROWS = 65536
N_ROW = 8
DEVICES = 32


def draw_harmonic(key, part):
    pairs_total = (NMAX + 1) ** 2 - 4
    lowest = NMAX * NMAX - 4
    first_key, second_key = jax.random.split(jax.random.fold_in(key, 17))
    others = jax.random.permutation(first_key, pairs_total - 2)[:PANEL - 2].astype(jnp.int32)
    others = jnp.where(others >= lowest, others + 1, others).astype(jnp.int32)
    chosen = jnp.concatenate([jnp.array([lowest, pairs_total - 1], jnp.int32), others])
    chosen = chosen[jax.random.permutation(second_key, PANEL)]
    levels = jnp.arange(3, NMAX + 1, dtype=jnp.int32)
    degree = 2 + jnp.sum(((levels * levels - 4)[None, :] <= chosen[:, None]).astype(jnp.int32), axis=1)
    order_index = chosen - (degree * degree - 4) - degree
    return jnp.stack([degree, order_index]).astype(jnp.int32)


def with_ends(values, key, low, largest):
    longest = values.shape.index(max(values.shape))
    spots = []
    for shift in (0, 1):
        where = [jax.random.randint(jax.random.fold_in(key, axis), (), 0, length) for axis, length in enumerate(values.shape)]
        where[longest] = (where[longest] + shift) % values.shape[longest]
        spots.append(tuple(where))
    return values.at[spots[0]].set(low).at[spots[1]].set(largest)


def level_of(stream_key, shape, cuts, smallest, top_value):
    def one(dim, parts):
        steps = jax.random.uniform(jax.random.fold_in(jax.random.fold_in(stream_key, 6), dim), (parts,), jnp.float32, smallest / len(cuts), top_value / len(cuts))
        return jnp.repeat(jnp.exp(steps), shape[dim] // parts).reshape((-1,) + (1,) * (len(shape) - dim - 1))

    gain = one(*cuts[0])
    for cut in cuts[1:]:
        gain = gain * one(*cut)
    return gain


def normal_values(stream_key, extent, deviation, bound, shards=(), kind=jnp.bfloat16):
    drawn = deviation * jax.random.normal(stream_key, extent, jnp.float32)
    if shards:
        drawn = drawn * level_of(stream_key, extent, shards, -0.22, 0.18)
    return jnp.clip(drawn, -bound, bound).astype(kind)


def setup_inputs(seed: int = 0) -> dict:
    splits = jax.random.split(jax.random.key(seed), 7)
    colatitude = jnp.clip(0.05 + 3.04 * jax.random.uniform(splits[0], (ROWS,), jnp.float32) ** level_of(splits[0], (ROWS,), ((0, 32),), -0.2, 0.2), 0.05, 3.09)
    longitude = jnp.clip(jax.random.uniform(splits[1], (ROWS,), jnp.float32, -3.140625, 3.140625), -3.140625, 3.140625)
    observed = normal_values(splits[2], (2, ROWS), 1.0, 6.0, ((1, 32),))
    filter_taps = normal_values(splits[3], (2, TAPS), TAPS ** -0.5, 0.375)
    segment_start = with_ends((jax.random.randint(splits[4], (ROWS,), 0, ROWS_DEV) < 2).astype(jnp.int32), jax.random.fold_in(splits[4], 1), 0, 1)
    harmonic = draw_harmonic(jax.random.fold_in(splits[6], 71), 0)
    return {"colatitude": colatitude, "longitude": longitude, "observed": observed, "filter_taps": filter_taps, "segment_start": segment_start, "harmonic": harmonic}


def design_rows(colatitude, longitude, harmonic):
    degree = harmonic[0].astype(jnp.float32)
    order_index = harmonic[1]
    polar_angle = colatitude[:, None] * degree[None, :]
    azimuth = longitude[:, None] * jnp.abs(order_index).astype(jnp.float32)[None, :]
    azimuth_wave = jnp.where(order_index[None, :] >= 0, jnp.cos(azimuth), jnp.sin(azimuth))
    radial = (jnp.cos(polar_angle) * azimuth_wave).astype(jnp.bfloat16)
    along = (jnp.sin(polar_angle) * azimuth_wave).astype(jnp.bfloat16)
    return radial, along


def reference(colatitude, longitude, observed, filter_taps, segment_start, harmonic):
    halo_rows = TAPS - 1
    group_rows = ROWS_DEV * N_ROW
    segment = jnp.cumsum(segment_start).astype(jnp.int32)
    colat_pad = jnp.concatenate([jnp.zeros((halo_rows,), colatitude.dtype), colatitude])
    long_pad = jnp.concatenate([jnp.zeros((halo_rows,), longitude.dtype), longitude])
    obs_pad = jnp.concatenate([jnp.zeros((2, halo_rows), observed.dtype), observed], axis=1)
    seg_pad = jnp.concatenate([jnp.full((halo_rows,), -1, jnp.int32), segment])
    position = jnp.arange(ROWS + halo_rows, dtype=jnp.int32) - halo_rows
    group_index = jnp.where(position >= 0, position // group_rows, -1).astype(jnp.int32)
    row_idx = jnp.arange(TAPS, dtype=jnp.int32)[:, None]
    col_idx = jnp.arange(2 * TAPS - 1, dtype=jnp.int32)[None, :]
    tap_lag = row_idx + TAPS - 1 - col_idx
    inside = (tap_lag >= 0) & (tap_lag <= TAPS - 1)
    clipped = jnp.clip(tap_lag, 0, TAPS - 1)
    toeplitz = jnp.where(inside[None], filter_taps[:, clipped], jnp.zeros((), filter_taps.dtype))

    def one_block(carried, number):
        normal_acc, rhs_acc = carried
        block_base = (number * ROWS_DEV).astype(jnp.int32)
        span = ROWS_DEV + halo_rows
        win_colat = lax.dynamic_slice_in_dim(colat_pad, block_base, span)
        win_long = lax.dynamic_slice_in_dim(long_pad, block_base, span)
        win_seg = lax.dynamic_slice_in_dim(seg_pad, block_base, span)
        win_group = lax.dynamic_slice_in_dim(group_index, block_base, span)
        win_obs = lax.dynamic_slice_in_dim(obs_pad, block_base, span, 1)
        fields = design_rows(win_colat, win_long, harmonic)
        for component in range(2):
            pieces = []
            signal_pieces = []
            for block_index in range(ROWS_DEV // TAPS):
                block_low = block_index * TAPS
                in_seg = win_seg[block_low:block_low + 2 * TAPS - 1]
                out_seg = win_seg[block_low + halo_rows:block_low + halo_rows + TAPS]
                in_group = win_group[block_low:block_low + 2 * TAPS - 1]
                out_group = win_group[block_low + halo_rows:block_low + halo_rows + TAPS]
                valid_mask = (out_seg[:, None] == in_seg[None, :]) & (out_group[:, None] == in_group[None, :])
                matrix = jnp.where(valid_mask, toeplitz[component], jnp.zeros((), toeplitz.dtype))
                pieces.append(jnp.dot(matrix, fields[component][block_low:block_low + 2 * TAPS - 1], preferred_element_type=jnp.float32).astype(jnp.bfloat16))
                signal_pieces.append(jnp.dot(matrix, win_obs[component, block_low:block_low + 2 * TAPS - 1], preferred_element_type=jnp.float32).astype(jnp.bfloat16))
            filtered = jnp.concatenate(pieces, axis=0)
            filtered_signal = jnp.concatenate(signal_pieces, axis=0)
            normal_acc = normal_acc + jnp.dot(filtered.T, filtered, preferred_element_type=jnp.float32)
            rhs_acc = rhs_acc + jnp.dot(filtered_signal, filtered, preferred_element_type=jnp.float32)
        return (normal_acc, rhs_acc), None

    start_state = (jnp.zeros((PANEL, PANEL), jnp.float32), jnp.zeros((PANEL,), jnp.float32))
    (gram, right_side), _ = lax.scan(one_block, start_state, jnp.arange(DEVICES, dtype=jnp.int32))
    same_index = jnp.arange(PANEL, dtype=jnp.int32)[:, None] == jnp.arange(PANEL, dtype=jnp.int32)[None, :]
    normal = jnp.where(same_index, jnp.zeros((), gram.dtype), gram) * (ROWS ** -0.5)
    diagonal = jnp.diagonal(gram) * (1.0 / ROWS)
    return normal, right_side * (ROWS ** -0.5), diagonal
```

```python
import functools
import math

import jax
import jax.numpy as jnp
from jax import lax
from jax.experimental import pallas as pl
from jax.experimental.pallas import tpu as pltpu
from jax.sharding import PartitionSpec as P

F32 = jnp.float32
BF16 = jnp.bfloat16
LANES = 128
EXTRA = 16
CHUNK = 64
SIN_C = (4.442866325378418, -7.307384967803955, 3.594230890274048, -0.7829042077064514)
COS_C = (1.41420316696167, -6.977553367614746, 5.714066982269287, -1.7246402502059937)
TURN_HIGH = 2608.0 / 16384.0
TURN_LOW = 1.0 / (2.0 * math.pi) - TURN_HIGH
FUSED = True


def poly(u, coefficients):
    total = coefficients[-1]
    for c in coefficients[-2::-1]:
        total = total * u + c
    return total


def turns(angle):
    head = jnp.round(angle * 1024.0) * (1.0 / 1024.0)
    tail = angle - head
    coarse = head * TURN_HIGH
    high = jnp.round(coarse * 32768.0) * (1.0 / 32768.0)
    low = (coarse - high) + (head * TURN_LOW + tail * (TURN_HIGH + TURN_LOW))
    return high, low


def local_kernel(
    fused, n_grp, n_row, blocks, taps_n, width,
    col_ref, lon_ref, obs_ref, taps_ref, seg_ref, har_ref, *refs,
):
    if fused:
        (out_ref, small_ref, design, filt, table, matrix, lab_col, lab, waves, gram,
         halo_send, halo, sa, ra, sb, rb, sc, rc, sd, rd, rs, rr, rz, send_sem, recv_sem) = refs
    else:
        (halo, gram, small_ref, design, filt, table, matrix, lab_col, lab, waves) = refs
    per = taps_n // LANES
    col_tiles = width // LANES
    row_index = lax.axis_index("row")
    grp_index = lax.axis_index("grp")

    if fused:
        core = lax.rem(row_index, 2)
        z = row_index // 2
        y = grp_index // 2
        x = lax.rem(grp_index, 2)
        n_z = n_row // 2
        twin = (grp_index, row_index + 1 - 2 * core)
        y_peer = (lax.rem(grp_index + 2, 4), row_index)
        x_peer = (grp_index + 1 - 2 * x, row_index)
        z_peers = [(grp_index, lax.rem(row_index + 2 * k, n_row)) for k in range(1, n_z)]
        after = (grp_index, lax.rem(row_index + 1, n_row))
        before = (grp_index, lax.rem(row_index + n_row - 1, n_row))
        greeted = [twin, y_peer, x_peer, after, before] + z_peers
        barrier = pltpu.get_barrier_semaphore()
        for peer in greeted:
            pl.semaphore_signal(barrier, inc=1, device_id=peer, device_id_type=pl.DeviceIdType.MESH)
        pl.semaphore_wait(barrier, len(greeted))

        def copy(src, dst, number, peer):
            c = pltpu.make_async_remote_copy(
                src_ref=src, dst_ref=dst,
                send_sem=send_sem.at[number], recv_sem=recv_sem.at[number],
                device_id=peer, device_id_type=pl.DeviceIdType.MESH,
            )
            c.start()
            return c

        last = blocks * per - per
        halo_send[0:per] = col_ref[last:last + per]
        halo_send[per:2 * per] = lon_ref[last:last + per]
        halo_send[2 * per:3 * per] = seg_ref[last:last + per].astype(F32)
        for c in range(2):
            for p in range(per):
                at = (last + p) * LANES
                halo_send[(3 + c) * per + p:(3 + c) * per + p + 1] = obs_ref[
                    c:c + 1, at:at + LANES].astype(F32)
        halo_send[5 * per:] = jnp.zeros((halo_send.shape[0] - 5 * per, LANES), F32)
        halo_copy = copy(halo_send, halo, 0, after)

    degree = har_ref[0:1, :].astype(F32)
    order = har_ref[1:2, :]
    size = jnp.abs(order).astype(F32)
    phase = jnp.where(order >= 0, 0.0, -0.25).astype(F32)
    for number, values in enumerate((degree, size, phase)):
        for t in range(col_tiles):
            here = slice(t * LANES, (t + 1) * LANES)
            waves[number, here, :] = jnp.broadcast_to(values[:, here], (LANES, LANES)).T

    j = lax.broadcasted_iota(jnp.int32, (taps_n, taps_n), 0)
    i = lax.broadcasted_iota(jnp.int32, (taps_n, taps_n), 1)
    for c in range(2):
        row = jnp.broadcast_to(taps_ref[c:c + 1, :].astype(F32), (taps_n, taps_n))
        around = pltpu.roll(row, 0, 1, stride=1, stride_axis=0)
        table[c, 0:taps_n, :] = jnp.where(i < j, around, 0.0)
        table[c, taps_n:, :] = jnp.where(i >= j, around, 0.0)

    upper = (
        lax.broadcasted_iota(jnp.int32, (LANES, LANES), 0)
        <= lax.broadcasted_iota(jnp.int32, (LANES, LANES), 1)
    ).astype(BF16)
    within = jnp.dot(seg_ref[...].astype(F32).astype(BF16), upper, preferred_element_type=F32)
    offset = jnp.zeros((1, 1), F32)
    for r in range(blocks * per):
        lab[per + r:per + r + 1, :] = within[r:r + 1] + offset
        offset = offset + within[r:r + 1, LANES - 1:]

    def label_columns(tile):
        at = pl.multiple_of(tile * LANES, LANES)
        lab_col[pl.ds(at, LANES), :] = jnp.broadcast_to(lab[pl.ds(tile, 1), :], (LANES, LANES)).T

    @pl.loop(per, (blocks + 1) * per)
    def _(tile):
        label_columns(tile)

    def design_tile(theta, phi, tile):
        at = pl.multiple_of(tile * LANES, LANES)
        theta_high, theta_low = turns(theta)
        phi_high, phi_low = turns(phi)

        @pl.loop(0, width // CHUNK)
        def _(chunk):
            rows = pl.ds(pl.multiple_of(chunk * CHUNK, CHUNK), CHUNK)
            n = waves[0, rows, :]
            m = waves[1, rows, :]
            a = n * theta_high
            a = (a - jnp.round(a)) + n * theta_low
            b = m * phi_high + waves[2, rows, :]
            b = (b - jnp.round(b)) + m * phi_low
            ua = a * a
            ub = b * b
            sin_a = a * poly(ua, SIN_C)
            cos_a = poly(ua, COS_C)
            sin_b = b * poly(ub, SIN_C)
            w = 1.0 - sin_b * sin_b
            design[0, rows, pl.ds(at, LANES)] = ((1.0 - sin_a * sin_a) * w).astype(BF16)
            design[1, rows, pl.ds(at, LANES)] = ((sin_a * cos_a) * w).astype(BF16)

    below = lax.broadcasted_iota(jnp.int32, (EXTRA, LANES), 0) == 0

    def signal_tile(values, c, tile):
        at = pl.multiple_of(tile * LANES, LANES)
        design[c, width:, pl.ds(at, LANES)] = jnp.where(
            below, jnp.broadcast_to(values, (EXTRA, LANES)), 0.0
        ).astype(BF16)

    @pl.loop(0, blocks * per)
    def _(tile):
        design_tile(col_ref[pl.ds(tile, 1), :], lon_ref[pl.ds(tile, 1), :], tile + per)
        for c in range(2):
            at = pl.multiple_of(tile * LANES, LANES)
            signal_tile(obs_ref[c:c + 1, pl.ds(at, LANES)].astype(F32), c, tile + per)

    if fused:
        halo_copy.wait()
    counts = jnp.dot(
        halo[2 * per:3 * per].astype(BF16), upper, preferred_element_type=F32
    )
    offset = jnp.zeros((1, 1), F32)
    rows = []
    for r in range(per):
        rows.append(counts[r:r + 1] + offset)
        offset = offset + counts[r:r + 1, LANES - 1:]
    first = row_index == 0
    for r in range(per):
        lab[r:r + 1, :] = jnp.where(first, -1.0, rows[r] - offset)
        label_columns(r)

    @pl.loop(0, per)
    def _(tile):
        design_tile(halo[pl.ds(tile, 1), :], halo[pl.ds(per + tile, 1), :], tile)
        for c in range(2):
            signal_tile(halo[pl.ds((3 + c) * per + tile, 1), :], c, tile)

    epochs = blocks * taps_n

    @pl.loop(0, blocks)
    def _(block):
        window = pl.multiple_of(block * taps_n, taps_n)
        for half in range(per):
            lanes = slice(half * LANES, (half + 1) * LANES)
            out_label = lab[pl.ds((block + 1) * per + half, 1), :]
            for part in range(2 * taps_n // LANES):
                at = slice(part * LANES, (part + 1) * LANES)
                same = lab_col[pl.ds(window + part * LANES, LANES), :] == out_label
                for c in range(2):
                    matrix[c, at, lanes] = jnp.where(same, table[c, at, lanes], 0.0).astype(BF16)
        for c in range(2):
            filt[:, pl.ds(pl.multiple_of(c * epochs + window, taps_n), taps_n)] = jnp.dot(
                design[c, :, pl.ds(window, 2 * taps_n)], matrix[c],
                preferred_element_type=F32,
            ).astype(BF16)

    half_width = width // 2
    half_tiles = half_width // LANES
    depth = min(1024, 2 * epochs)
    copies_a = []
    for half in range(2):
        gram[half * half_tiles:(half + 1) * half_tiles] = jnp.zeros(
            (half_tiles, width + EXTRA, LANES), F32
        )

        @pl.loop(0, 2 * epochs // depth)
        def _(step):
            at = pl.ds(pl.multiple_of(step * depth, depth), depth)
            part = lax.dot_general(
                filt[:, at], filt[half * half_width:(half + 1) * half_width, at],
                (((1,), (1,)), ((), ())), preferred_element_type=F32,
            )
            for t in range(half_tiles):
                gram[half * half_tiles + t] += part[:, t * LANES:(t + 1) * LANES]

        if fused:
            tile_rows = width // n_row
            for t in range(half * half_tiles, (half + 1) * half_tiles):
                for zz in range(n_z):
                    at = pl.multiple_of((2 * zz + 1 - core) * tile_rows, tile_rows)
                    sa[t, zz] = gram[t, pl.ds(at, tile_rows), :].astype(BF16)
            part = pl.ds(half * half_tiles, half_tiles)
            copies_a.append(copy(sa.at[part], ra.at[part], 1 + half, twin))

    eye = lax.broadcasted_iota(jnp.int32, (LANES, LANES), 0) == lax.broadcasted_iota(
        jnp.int32, (LANES, LANES), 1
    )
    small = []
    for t in range(col_tiles):
        small.append(gram[t, width:width + 1, :])
    for t in range(col_tiles):
        square = gram[t, t * LANES:(t + 1) * LANES, :]
        small.append(jnp.sum(jnp.where(eye, square, 0.0), axis=0, keepdims=True))
    if not fused:
        for r, row in enumerate(small):
            small_ref[r:r + 1, :] = row
        return

    for r, row in enumerate(small):
        rs[0, r:r + 1, :] = row
    small_a = copy(rs.at[0], rr.at[0], 3, twin)
    for c in copies_a:
        c.wait()
    for t in range(col_tiles):
        for zz in range(n_z):
            at = pl.multiple_of((2 * zz + core) * tile_rows, tile_rows)
            gram[t, pl.ds(zz * tile_rows, tile_rows), :] = gram[
                t, pl.ds(at, tile_rows), :] + ra[t, zz].astype(F32)

    def held(t, zz):
        return gram[t, pl.ds(pl.multiple_of(zz * tile_rows, tile_rows), tile_rows), :]

    def add(t, zz, values):
        at = pl.ds(pl.multiple_of(zz * tile_rows, tile_rows), tile_rows)
        gram[t, at, :] = gram[t, at, :] + values.astype(F32)

    z_half = n_z // 2
    for k in range(2):
        for q in range(z_half):
            sb[0, k, q] = held(2 * (1 - y) + k, q).astype(BF16)
            sb[1, k, q] = held(2 * k + 1 - x, z_half + q).astype(BF16)
    copies_b = [copy(sb.at[0], rb.at[0], 4, y_peer), copy(sb.at[1], rb.at[1], 5, x_peer)]
    small_a.wait()
    rs[1] = rs[0] + rr[0]
    small_b = copy(rs.at[1], rr.at[1], 6, y_peer)
    copies_b[0].wait()
    for q in range(z_half):
        sc[0, q] = (held(2 * y + 1 - x, q) + rb[0, 1 - x, q].astype(F32)).astype(BF16)
    copies_c = [copy(sc.at[0], rc.at[0], 7, x_peer)]
    copies_b[1].wait()
    for q in range(z_half):
        sc[1, q] = (held(2 * (1 - y) + x, z_half + q) + rb[1, 1 - y, q].astype(F32)).astype(BF16)
    copies_c.append(copy(sc.at[1], rc.at[1], 8, y_peer))
    for q in range(z_half):
        add(grp_index, q, rb[0, x, q])
        add(grp_index, z_half + q, rb[1, y, q])
    small_b.wait()
    rs[2] = rs[1] + rr[1]
    small_c = copy(rs.at[2], rr.at[2], 9, x_peer)
    for s in range(2):
        copies_c[s].wait()
        for q in range(z_half):
            add(grp_index, s * z_half + q, rc[s, q])
    copies_d = []
    for k in range(1, n_z):
        sd[k - 1] = held(grp_index, lax.rem(z + k, n_z)).astype(BF16)
        copies_d.append(copy(sd.at[k - 1], rd.at[k - 1], 9 + k, z_peers[k - 1]))
    small_c.wait()
    rz[z] = rs[2] + rr[2]
    small_d = []
    for k in range(1, n_z):
        small_d.append(copy(rz.at[z], rz.at[z], 8 + n_z + k, z_peers[k - 1]))
    total = held(grp_index, z)
    for k in range(1, n_z):
        copies_d[k - 1].wait()
        total = total + rd[k - 1].astype(F32)
    out_ref[...] = total
    for c in small_d:
        c.wait()
    total = rz[0]
    for zz in range(1, n_z):
        total = total + rz[zz]
    small_ref[...] = total


def on_device(colatitude, longitude, observed, filter_taps, segment_start, harmonic):
    rows_here = colatitude.shape[0]
    taps_n = filter_taps.shape[1]
    width = harmonic.shape[1]
    n_grp = lax.axis_size("grp")
    n_row = lax.axis_size("row")
    blocks = rows_here // taps_n
    per = taps_n // LANES
    tiles = width // LANES
    rows_total = rows_here * n_grp * n_row
    row_scale = 1.0 / rows_total
    gram_scale = 1.0 / math.sqrt(rows_total)
    fused = FUSED and n_grp == 4 and n_row == 8 and width == n_grp * LANES
    split = [a.reshape(rows_here // LANES, LANES) for a in (colatitude, longitude, segment_start)]
    inputs = [split[0], split[1], observed, filter_taps, split[2], harmonic]
    window = rows_here + taps_n
    scratch = [
        pltpu.VMEM((2, width + EXTRA, window), BF16),
        pltpu.VMEM((width + EXTRA, 2 * rows_here), BF16),
        pltpu.VMEM((2, 2 * taps_n, taps_n), F32),
        pltpu.VMEM((2, 2 * taps_n, taps_n), BF16),
        pltpu.VMEM((window, LANES), F32),
        pltpu.VMEM((window // LANES, LANES), F32),
        pltpu.VMEM((3, width, LANES), F32),
    ]
    gram_shape = (tiles, width + EXTRA, LANES)
    small_shape = jax.ShapeDtypeStruct((2 * tiles, LANES), F32)
    halo_shape = (8 * per, LANES)
    if fused:
        tile_rows = width // n_row
        n_z = n_row // 2
        tile = (tile_rows, LANES)
        copies = 9 + 2 * n_z
        scratch += [
            pltpu.VMEM(gram_shape, F32),
            pltpu.VMEM(halo_shape, F32),
            pltpu.VMEM(halo_shape, F32),
            pltpu.VMEM((tiles, n_z) + tile, BF16),
            pltpu.VMEM((tiles, n_z) + tile, BF16),
            pltpu.VMEM((2, 2, n_z // 2) + tile, BF16),
            pltpu.VMEM((2, 2, n_z // 2) + tile, BF16),
            pltpu.VMEM((2, n_z // 2) + tile, BF16),
            pltpu.VMEM((2, n_z // 2) + tile, BF16),
            pltpu.VMEM((n_z - 1,) + tile, BF16),
            pltpu.VMEM((n_z - 1,) + tile, BF16),
            pltpu.VMEM((3, 2 * tiles, LANES), F32),
            pltpu.VMEM((3, 2 * tiles, LANES), F32),
            pltpu.VMEM((n_z, 2 * tiles, LANES), F32),
            pltpu.SemaphoreType.DMA((copies,)),
            pltpu.SemaphoreType.DMA((copies,)),
        ]
        main_shape = jax.ShapeDtypeStruct((tile_rows, LANES), F32)
    else:
        last = rows_here // LANES - per
        pieces = [split[0][last:], split[1][last:], split[2][last:].astype(F32)]
        pieces.append(observed[:, rows_here - taps_n:].astype(F32).reshape(2 * per, LANES))
        pieces.append(jnp.zeros((3 * per, LANES), F32))
        pairs = [(k, k + 1) for k in range(n_row - 1)]
        inputs.append(lax.ppermute(jnp.concatenate(pieces), "row", pairs))
        main_shape = jax.ShapeDtypeStruct(gram_shape, F32)
    params = dict(vmem_limit_bytes=40 * 1024 * 1024)
    if fused:
        params.update(collective_id=0, has_side_effects=True)
    main, small = pl.pallas_call(
        functools.partial(local_kernel, fused, n_grp, n_row, blocks, taps_n, width),
        out_shape=(main_shape, small_shape),
        in_specs=[pl.BlockSpec(memory_space=pltpu.VMEM)] * len(inputs),
        out_specs=(pl.BlockSpec(memory_space=pltpu.VMEM),) * 2,
        scratch_shapes=scratch,
        compiler_params=pltpu.CompilerParams(**params),
        name="normal_equations",
    )(*inputs)
    if fused:
        normal = main
    else:
        gram = main[:, :width].transpose(1, 0, 2).reshape(width, width)
        owned = lax.psum_scatter(gram, "row", scatter_dimension=0, tiled=True)
        normal = lax.psum_scatter(owned, "grp", scatter_dimension=1, tiled=True)
        small = lax.psum(small, ("grp", "row"))
    row_at = lax.axis_index("row") * normal.shape[0] + lax.broadcasted_iota(
        jnp.int32, normal.shape, 0
    )
    col_at = lax.axis_index("grp") * normal.shape[1] + lax.broadcasted_iota(
        jnp.int32, normal.shape, 1
    )
    normal = jnp.where(row_at == col_at, 0.0, normal * gram_scale)
    right_side = small[:tiles].reshape(width) * gram_scale
    diagonal = small[tiles:].reshape(width) * row_scale
    return (normal, right_side, diagonal)


def solution(mesh):
    placed = (
        P(("grp", "row")),
        P(("grp", "row")),
        P(None, ("grp", "row")),
        P(),
        P(("grp", "row")),
        P(),
    )
    return jax.shard_map(
        on_device,
        mesh=mesh,
        in_specs=placed,
        out_specs=(P("row", "grp"), P(), P()),
        check_vma=False,
    )
```

```python
import functools
import math

import jax
import jax.numpy as jnp
from jax import lax
from jax.experimental import pallas as pl
from jax.experimental.pallas import tpu as pltpu
from jax.sharding import PartitionSpec as P

F32 = jnp.float32
BF16 = jnp.bfloat16
LANES = 128
EXTRA = 16
CHUNK = 64
SIN_C = (4.442866325378418, -7.307384967803955, 3.594230890274048, -0.7829042077064514)
COS_C = (1.41420316696167, -6.977553367614746, 5.714066982269287, -1.7246402502059937)
TURN_HIGH = 2608.0 / 16384.0
TURN_LOW = 1.0 / (2.0 * math.pi) - TURN_HIGH
FUSED = True


def poly(u, coefficients):
    total = coefficients[-1]
    for c in coefficients[-2::-1]:
        total = total * u + c
    return total


def turns(angle):
    head = jnp.round(angle * 1024.0) * (1.0 / 1024.0)
    tail = angle - head
    coarse = head * TURN_HIGH
    high = jnp.round(coarse * 32768.0) * (1.0 / 32768.0)
    low = (coarse - high) + (head * TURN_LOW + tail * (TURN_HIGH + TURN_LOW))
    return high, low


def local_kernel(
    fused, n_grp, n_row, blocks, taps_n, width,
    col_in, lon_in, obs_in, taps_in, seg_in, har_in, *refs,
):
    if fused:
        (out_ref, small_ref, col_ref, lon_ref, obs_got, taps_ref, seg_ref, har_ref, in_sem,
         obs_ref, fresh, window, filt, table, matrix, lab_col, lab, waves, gram,
         halo_send, halo, sa, ra, sb, rb, sc, rc, sd, rd, rs, rr, rz, send_sem, recv_sem) = refs
    else:
        (halo, gram, small_ref, col_ref, lon_ref, obs_got, taps_ref, seg_ref, har_ref, in_sem,
         obs_ref, fresh, window, filt, table, matrix, lab_col, lab, waves) = refs
    per = taps_n // LANES
    own = blocks * per
    col_tiles = width // LANES
    row_index = lax.axis_index("row")
    grp_index = lax.axis_index("grp")

    fetched = (
        (har_in, har_ref), (taps_in, taps_ref), (col_in, col_ref.at[0:own]),
        (lon_in, lon_ref.at[0:own]), (seg_in, seg_ref), (obs_in, obs_got),
    )
    fetches = [
        pltpu.make_async_copy(src, dst, in_sem.at[k]) for k, (src, dst) in enumerate(fetched)
    ]
    for fetch in fetches:
        fetch.start()

    if fused:
        core = lax.rem(row_index, 2)
        z = row_index // 2
        y = grp_index // 2
        x = lax.rem(grp_index, 2)
        n_z = n_row // 2
        twin = (grp_index, row_index + 1 - 2 * core)
        y_peer = (lax.rem(grp_index + 2, 4), row_index)
        x_peer = (grp_index + 1 - 2 * x, row_index)
        z_peers = [(grp_index, lax.rem(row_index + 2 * k, n_row)) for k in range(1, n_z)]
        after = (grp_index, lax.rem(row_index + 1, n_row))
        before = (grp_index, lax.rem(row_index + n_row - 1, n_row))
        greeted = [twin, y_peer, x_peer, after, before] + z_peers
        barrier = pltpu.get_barrier_semaphore()
        for peer in greeted:
            pl.semaphore_signal(barrier, inc=1, device_id=peer, device_id_type=pl.DeviceIdType.MESH)

        def copy(src, dst, number, peer):
            c = pltpu.make_async_remote_copy(
                src_ref=src, dst_ref=dst,
                send_sem=send_sem.at[number], recv_sem=recv_sem.at[number],
                device_id=peer, device_id_type=pl.DeviceIdType.MESH,
            )
            c.start()
            return c

    for fetch in fetches:
        fetch.wait()
    obs_ref[:, 0:own * LANES] = obs_got[...].astype(F32)

    if fused:
        last = own - per
        halo_send[0:per] = col_ref[last:last + per]
        halo_send[per:2 * per] = lon_ref[last:last + per]
        halo_send[2 * per:3 * per] = seg_ref[last:last + per].astype(F32)
        for c in range(2):
            for p in range(per):
                at = (last + p) * LANES
                halo_send[(3 + c) * per + p:(3 + c) * per + p + 1] = obs_ref[
                    c:c + 1, at:at + LANES]
        halo_send[5 * per:] = jnp.zeros((halo_send.shape[0] - 5 * per, LANES), F32)
        pl.semaphore_wait(barrier, len(greeted))
        halo_copy = copy(halo_send, halo, 0, after)

    degree = har_ref[0:1, :].astype(F32)
    order = har_ref[1:2, :]
    size = jnp.abs(order).astype(F32)
    phase = jnp.where(order >= 0, 0.0, -0.25).astype(F32)
    for number, values in enumerate((degree, size, phase)):
        for t in range(col_tiles):
            here = slice(t * LANES, (t + 1) * LANES)
            waves[number, here, :] = jnp.broadcast_to(values[:, here], (LANES, LANES)).T

    below = lax.broadcasted_iota(jnp.int32, (EXTRA, LANES), 0) == 0

    def design_block(slot):
        for half in range(per):
            tile = slot * per + half
            lanes = slice(half * LANES, (half + 1) * LANES)
            theta_high, theta_low = turns(col_ref[pl.ds(tile, 1), :])
            phi_high, phi_low = turns(lon_ref[pl.ds(tile, 1), :])
            for chunk in range(width // CHUNK):
                rows = slice(chunk * CHUNK, (chunk + 1) * CHUNK)
                n = waves[0, rows, :]
                m = waves[1, rows, :]
                a = n * theta_high
                a = (a - jnp.round(a)) + n * theta_low
                b = m * phi_high + waves[2, rows, :]
                b = (b - jnp.round(b)) + m * phi_low
                ua = a * a
                ub = b * b
                sin_a = a * poly(ua, SIN_C)
                cos_a = poly(ua, COS_C)
                sin_b = b * poly(ub, SIN_C)
                w = 1.0 - sin_b * sin_b
                fresh[0, rows, lanes] = ((1.0 - sin_a * sin_a) * w).astype(BF16)
                fresh[1, rows, lanes] = ((sin_a * cos_a) * w).astype(BF16)
            at = pl.multiple_of(tile * LANES, LANES)
            for c in range(2):
                values = obs_ref[c:c + 1, pl.ds(at, LANES)]
                fresh[c, width:, lanes] = jnp.where(
                    below, jnp.broadcast_to(values, (EXTRA, LANES)), 0.0
                ).astype(BF16)

    def shift():
        window[:, :, taps_n:] = window[:, :, :taps_n]
        window[:, :, :taps_n] = fresh[...]

    window[:, :, :taps_n] = jnp.zeros((2, width + EXTRA, taps_n), BF16)

    @pl.loop(0, 2)
    def _(step):
        design_block(blocks - 1 - step)
        shift()

    j = lax.broadcasted_iota(jnp.int32, (taps_n, taps_n), 0)
    i = lax.broadcasted_iota(jnp.int32, (taps_n, taps_n), 1)
    for c in range(2):
        row = jnp.broadcast_to(taps_ref[c:c + 1, :].astype(F32), (taps_n, taps_n))
        around = pltpu.roll(row, 0, 1, stride=1, stride_axis=0)
        table[c, 0:taps_n, :] = jnp.where(i < j, around, 0.0)
        table[c, taps_n:, :] = jnp.where(i >= j, around, 0.0)

    upper = (
        lax.broadcasted_iota(jnp.int32, (LANES, LANES), 0)
        <= lax.broadcasted_iota(jnp.int32, (LANES, LANES), 1)
    ).astype(BF16)

    def running(flags, count):
        within = jnp.dot(flags.astype(BF16), upper, preferred_element_type=F32)
        offset = jnp.zeros((1, 1), F32)
        rows = []
        for r in range(count):
            rows.append(within[r:r + 1] + offset)
            offset = offset + within[r:r + 1, LANES - 1:]
        return rows, offset

    rows, _ = running(seg_ref[...].astype(F32), own)
    for r in range(own):
        lab[r:r + 1, :] = rows[r]
    if fused:
        halo_copy.wait()
    rows, total = running(halo[2 * per:3 * per], per)
    first = row_index == 0
    for r in range(per):
        lab[own + r:own + r + 1, :] = jnp.where(first, -1.0, rows[r] - total)
        for c in range(2):
            at = (3 + c) * per + r
            obs_ref[c:c + 1, (own + r) * LANES:(own + r + 1) * LANES] = halo[at:at + 1]
    col_ref[own:own + per] = halo[0:per]
    lon_ref[own:own + per] = halo[per:2 * per]

    @pl.loop(0, own + per)
    def _(tile):
        at = pl.multiple_of(tile * LANES, LANES)
        lab_col[pl.ds(at, LANES), :] = jnp.broadcast_to(lab[pl.ds(tile, 1), :], (LANES, LANES)).T

    half_width = width // 2
    half_tiles = half_width // LANES
    gram[...] = jnp.zeros(gram.shape, F32)

    def filter_block(block):
        slots = (lax.rem(block + blocks, blocks + 1), block)
        for half in range(per):
            lanes = slice(half * LANES, (half + 1) * LANES)
            out_label = lab[pl.ds(block * per + half, 1), :]
            for part in range(2 * per):
                at = slice(part * LANES, (part + 1) * LANES)
                tile = slots[part // per] * per + part % per
                got = lab_col[pl.ds(pl.multiple_of(tile * LANES, LANES), LANES), :]
                same = got == out_label
                for c in range(2):
                    matrix[c, at, lanes] = jnp.where(same, table[c, at, lanes], 0.0).astype(BF16)
        for c in range(2):
            filt[:, c * taps_n:(c + 1) * taps_n] = jnp.dot(
                window[c], matrix[c], preferred_element_type=F32
            ).astype(BF16)

    def gram_half(half):
        from_row = half * half_width
        part = lax.dot_general(
            filt[from_row:, :], filt[from_row:from_row + half_width, :],
            (((1,), (1,)), ((), ())), preferred_element_type=F32,
        )
        for t in range(half_tiles):
            gram[half * half_tiles + t, from_row:, :] += part[:, t * LANES:(t + 1) * LANES]

    @pl.loop(0, blocks - 1)
    def _(step):
        block = blocks - 1 - step
        design_block(lax.rem(block - 2 + blocks + 1, blocks + 1))
        filter_block(block)
        gram_half(0)
        gram_half(1)
        shift()

    filter_block(0)
    copies_a = []
    for half in range(2):
        gram_half(half)
        if half == 1:
            for t in range(half_tiles):
                for q in range(half_tiles):
                    gram[half_tiles + t, q * LANES:(q + 1) * LANES, :] = gram[
                        q, half_width + t * LANES:half_width + (t + 1) * LANES, :].T
        if fused:
            tile_rows = width // n_row
            for t in range(half * half_tiles, (half + 1) * half_tiles):
                for zz in range(n_z):
                    at = pl.multiple_of((2 * zz + 1 - core) * tile_rows, tile_rows)
                    sa[t, zz] = gram[t, pl.ds(at, tile_rows), :].astype(BF16)
            part = pl.ds(half * half_tiles, half_tiles)
            copies_a.append(copy(sa.at[part], ra.at[part], 1 + half, twin))

    eye = lax.broadcasted_iota(jnp.int32, (LANES, LANES), 0) == lax.broadcasted_iota(
        jnp.int32, (LANES, LANES), 1
    )
    small = []
    for t in range(col_tiles):
        small.append(gram[t, width:width + 1, :])
    for t in range(col_tiles):
        square = gram[t, t * LANES:(t + 1) * LANES, :]
        small.append(jnp.sum(jnp.where(eye, square, 0.0), axis=0, keepdims=True))
    if not fused:
        for r, row in enumerate(small):
            small_ref[r:r + 1, :] = row
        return

    for r, row in enumerate(small):
        rs[0, r:r + 1, :] = row
    small_a = copy(rs.at[0], rr.at[0], 3, twin)
    for c in copies_a:
        c.wait()
    for t in range(col_tiles):
        for zz in range(n_z):
            at = pl.multiple_of((2 * zz + core) * tile_rows, tile_rows)
            gram[t, pl.ds(zz * tile_rows, tile_rows), :] = gram[
                t, pl.ds(at, tile_rows), :] + ra[t, zz].astype(F32)

    def held(t, zz):
        return gram[t, pl.ds(pl.multiple_of(zz * tile_rows, tile_rows), tile_rows), :]

    def add(t, zz, values):
        at = pl.ds(pl.multiple_of(zz * tile_rows, tile_rows), tile_rows)
        gram[t, at, :] = gram[t, at, :] + values.astype(F32)

    z_half = n_z // 2
    for k in range(2):
        for q in range(z_half):
            sb[0, k, q] = held(2 * (1 - y) + k, q).astype(BF16)
            sb[1, k, q] = held(2 * k + 1 - x, z_half + q).astype(BF16)
    copies_b = [copy(sb.at[0], rb.at[0], 4, y_peer), copy(sb.at[1], rb.at[1], 5, x_peer)]
    small_a.wait()
    rs[1] = rs[0] + rr[0]
    small_b = copy(rs.at[1], rr.at[1], 6, y_peer)
    copies_b[0].wait()
    for q in range(z_half):
        sc[0, q] = (held(2 * y + 1 - x, q) + rb[0, 1 - x, q].astype(F32)).astype(BF16)
    copies_c = [copy(sc.at[0], rc.at[0], 7, x_peer)]
    copies_b[1].wait()
    for q in range(z_half):
        sc[1, q] = (held(2 * (1 - y) + x, z_half + q) + rb[1, 1 - y, q].astype(F32)).astype(BF16)
    copies_c.append(copy(sc.at[1], rc.at[1], 8, y_peer))
    for q in range(z_half):
        add(grp_index, q, rb[0, x, q])
        add(grp_index, z_half + q, rb[1, y, q])
    small_b.wait()
    rs[2] = rs[1] + rr[1]
    small_c = copy(rs.at[2], rr.at[2], 9, x_peer)
    for s in range(2):
        copies_c[s].wait()
        for q in range(z_half):
            add(grp_index, s * z_half + q, rc[s, q])
    copies_d = []
    for k in range(1, n_z):
        sd[k - 1] = held(grp_index, lax.rem(z + k, n_z)).astype(BF16)
        copies_d.append(copy(sd.at[k - 1], rd.at[k - 1], 9 + k, z_peers[k - 1]))
    small_c.wait()
    rz[z] = rs[2] + rr[2]
    small_d = []
    for k in range(1, n_z):
        small_d.append(copy(rz.at[z], rz.at[z], 8 + n_z + k, z_peers[k - 1]))
    total = held(grp_index, z)
    for k in range(1, n_z):
        copies_d[k - 1].wait()
        total = total + rd[k - 1].astype(F32)
    out_ref[...] = total
    for c in small_d:
        c.wait()
    total = rz[0]
    for zz in range(1, n_z):
        total = total + rz[zz]
    small_ref[...] = total


def on_device(colatitude, longitude, observed, filter_taps, segment_start, harmonic):
    rows_here = colatitude.shape[0]
    taps_n = filter_taps.shape[1]
    width = harmonic.shape[1]
    n_grp = lax.axis_size("grp")
    n_row = lax.axis_size("row")
    blocks = rows_here // taps_n
    per = taps_n // LANES
    tiles = width // LANES
    rows_total = rows_here * n_grp * n_row
    row_scale = 1.0 / rows_total
    gram_scale = 1.0 / math.sqrt(rows_total)
    fused = FUSED and n_grp == 4 and n_row == 8 and width == n_grp * LANES
    split = [a.reshape(rows_here // LANES, LANES) for a in (colatitude, longitude, segment_start)]
    inputs = [split[0], split[1], observed, filter_taps, split[2], harmonic]
    window = rows_here + taps_n
    scratch = [
        pltpu.VMEM((window // LANES, LANES), F32),
        pltpu.VMEM((window // LANES, LANES), F32),
        pltpu.VMEM(observed.shape, observed.dtype),
        pltpu.VMEM(filter_taps.shape, filter_taps.dtype),
        pltpu.VMEM((rows_here // LANES, LANES), segment_start.dtype),
        pltpu.VMEM(harmonic.shape, harmonic.dtype),
        pltpu.SemaphoreType.DMA((6,)),
        pltpu.VMEM((2, window), F32),
        pltpu.VMEM((2, width + EXTRA, taps_n), BF16),
        pltpu.VMEM((2, width + EXTRA, 2 * taps_n), BF16),
        pltpu.VMEM((width + EXTRA, 2 * taps_n), BF16),
        pltpu.VMEM((2, 2 * taps_n, taps_n), F32),
        pltpu.VMEM((2, 2 * taps_n, taps_n), BF16),
        pltpu.VMEM((window, LANES), F32),
        pltpu.VMEM((window // LANES, LANES), F32),
        pltpu.VMEM((3, width, LANES), F32),
    ]
    gram_shape = (tiles, width + EXTRA, LANES)
    small_shape = jax.ShapeDtypeStruct((2 * tiles, LANES), F32)
    halo_shape = (8 * per, LANES)
    if fused:
        tile_rows = width // n_row
        n_z = n_row // 2
        tile = (tile_rows, LANES)
        copies = 9 + 2 * n_z
        scratch += [
            pltpu.VMEM(gram_shape, F32),
            pltpu.VMEM(halo_shape, F32),
            pltpu.VMEM(halo_shape, F32),
            pltpu.VMEM((tiles, n_z) + tile, BF16),
            pltpu.VMEM((tiles, n_z) + tile, BF16),
            pltpu.VMEM((2, 2, n_z // 2) + tile, BF16),
            pltpu.VMEM((2, 2, n_z // 2) + tile, BF16),
            pltpu.VMEM((2, n_z // 2) + tile, BF16),
            pltpu.VMEM((2, n_z // 2) + tile, BF16),
            pltpu.VMEM((n_z - 1,) + tile, BF16),
            pltpu.VMEM((n_z - 1,) + tile, BF16),
            pltpu.VMEM((3, 2 * tiles, LANES), F32),
            pltpu.VMEM((3, 2 * tiles, LANES), F32),
            pltpu.VMEM((n_z, 2 * tiles, LANES), F32),
            pltpu.SemaphoreType.DMA((copies,)),
            pltpu.SemaphoreType.DMA((copies,)),
        ]
        main_shape = jax.ShapeDtypeStruct((tile_rows, LANES), F32)
    else:
        last = rows_here // LANES - per
        pieces = [split[0][last:], split[1][last:], split[2][last:].astype(F32)]
        pieces.append(observed[:, rows_here - taps_n:].astype(F32).reshape(2 * per, LANES))
        pieces.append(jnp.zeros((3 * per, LANES), F32))
        pairs = [(k, k + 1) for k in range(n_row - 1)]
        inputs.append(lax.ppermute(jnp.concatenate(pieces), "row", pairs))
        main_shape = jax.ShapeDtypeStruct(gram_shape, F32)
    params = dict(vmem_limit_bytes=48 * 1024 * 1024)
    if fused:
        params.update(collective_id=0, has_side_effects=True)
    main, small = pl.pallas_call(
        functools.partial(local_kernel, fused, n_grp, n_row, blocks, taps_n, width),
        out_shape=(main_shape, small_shape),
        in_specs=[pl.BlockSpec(memory_space=pltpu.HBM)] * 6
        + [pl.BlockSpec(memory_space=pltpu.VMEM)] * (len(inputs) - 6),
        out_specs=(pl.BlockSpec(memory_space=pltpu.VMEM),) * 2,
        scratch_shapes=scratch,
        compiler_params=pltpu.CompilerParams(**params),
        name="normal_equations",
    )(*inputs)
    if fused:
        normal = main
    else:
        gram = main[:, :width].transpose(1, 0, 2).reshape(width, width)
        owned = lax.psum_scatter(gram, "row", scatter_dimension=0, tiled=True)
        normal = lax.psum_scatter(owned, "grp", scatter_dimension=1, tiled=True)
        small = lax.psum(small, ("grp", "row"))
    row_at = lax.axis_index("row") * normal.shape[0] + lax.broadcasted_iota(
        jnp.int32, normal.shape, 0
    )
    col_at = lax.axis_index("grp") * normal.shape[1] + lax.broadcasted_iota(
        jnp.int32, normal.shape, 1
    )
    normal = jnp.where(row_at == col_at, 0.0, normal * gram_scale)
    right_side = small[:tiles].reshape(width) * gram_scale
    diagonal = small[tiles:].reshape(width) * row_scale
    return (normal, right_side, diagonal)


def solution(mesh):
    placed = (
        P(("grp", "row")),
        P(("grp", "row")),
        P(None, ("grp", "row")),
        P(),
        P(("grp", "row")),
        P(),
    )
    return jax.shard_map(
        on_device,
        mesh=mesh,
        in_specs=placed,
        out_specs=(P("row", "grp"), P(), P()),
        check_vma=False,
    )
```

```python
import functools
import math

import jax
import jax.numpy as jnp
from jax import lax
from jax.experimental import pallas as pl
from jax.experimental.pallas import tpu as pltpu
from jax.sharding import PartitionSpec as P

F32 = jnp.float32
BF16 = jnp.bfloat16
LANES = 128
EXTRA = 16
CHUNK = 64
SIN_C = (4.442866325378418, -7.307384967803955, 3.594230890274048, -0.7829042077064514)
COS_C = (1.41420316696167, -6.977553367614746, 5.714066982269287, -1.7246402502059937)
TURN_HIGH = 2608.0 / 16384.0
TURN_LOW = 1.0 / (2.0 * math.pi) - TURN_HIGH
FUSED = True


def poly(u, coefficients):
    total = coefficients[-1]
    for c in coefficients[-2::-1]:
        total = total * u + c
    return total


def nearest(x):
    return (x + 12582912.0) - 12582912.0


def spread(columns, k):
    return jnp.broadcast_to(columns[:, k:k + 1], (LANES, LANES))


def turns(angle):
    head = nearest(angle * 1024.0) * (1.0 / 1024.0)
    tail = angle - head
    coarse = head * TURN_HIGH
    high = nearest(coarse * 32768.0) * (1.0 / 32768.0)
    low = (coarse - high) + (head * TURN_LOW + tail * (TURN_HIGH + TURN_LOW))
    return high, low


def local_kernel(
    fused, n_grp, n_row, blocks, taps_n, width, gram_scale, row_scale,
    col_in, lon_in, obs_in, taps_in, seg_in, har_in, *refs,
):
    if fused:
        (out_ref, small_ref, col_ref, lon_ref, obs_got, taps_ref, seg_ref, har_ref, in_sem,
         obs_ref, fresh, window, filt, table, matrix, lab_col, lab, waves, turned, gram,
         halo_send, halo, sa, ra, sb, rb, sc, rc, sd, rd, rs, rr, rz, send_sem, recv_sem) = refs
    else:
        (halo, gram, small_ref, col_ref, lon_ref, obs_got, taps_ref, seg_ref, har_ref, in_sem,
         obs_ref, fresh, window, filt, table, matrix, lab_col, lab, waves, turned) = refs
    per = taps_n // LANES
    own = blocks * per
    col_tiles = width // LANES
    row_index = lax.axis_index("row")
    grp_index = lax.axis_index("grp")

    fetched = (
        (har_in, har_ref), (taps_in, taps_ref), (col_in, col_ref.at[0:own]),
        (lon_in, lon_ref.at[0:own]), (seg_in, seg_ref), (obs_in, obs_got),
    )
    fetches = [
        pltpu.make_async_copy(src, dst, in_sem.at[k]) for k, (src, dst) in enumerate(fetched)
    ]
    for fetch in fetches:
        fetch.start()

    if fused:
        core = lax.rem(row_index, 2)
        z = row_index // 2
        y = grp_index // 2
        x = lax.rem(grp_index, 2)
        n_z = n_row // 2
        twin = (grp_index, row_index + 1 - 2 * core)
        y_peer = (lax.rem(grp_index + 2, 4), row_index)
        x_peer = (grp_index + 1 - 2 * x, row_index)
        z_peers = [(grp_index, lax.rem(row_index + 2 * k, n_row)) for k in range(1, n_z)]
        after = (grp_index, lax.rem(row_index + 1, n_row))
        before = (grp_index, lax.rem(row_index + n_row - 1, n_row))
        greeted = [twin, y_peer, x_peer, after, before] + z_peers
        barrier = pltpu.get_barrier_semaphore()
        for peer in greeted:
            pl.semaphore_signal(barrier, inc=1, device_id=peer, device_id_type=pl.DeviceIdType.MESH)

        def copy(src, dst, number, peer):
            c = pltpu.make_async_remote_copy(
                src_ref=src, dst_ref=dst,
                send_sem=send_sem.at[number], recv_sem=recv_sem.at[number],
                device_id=peer, device_id_type=pl.DeviceIdType.MESH,
            )
            c.start()
            return c

    for fetch in fetches:
        fetch.wait()
    obs_ref[:, 0:own * LANES] = obs_got[...].astype(F32)

    if fused:
        last = own - per
        halo_send[0:per] = col_ref[last:last + per]
        halo_send[per:2 * per] = lon_ref[last:last + per]
        halo_send[2 * per:3 * per] = seg_ref[last:last + per].astype(F32)
        for c in range(2):
            for p in range(per):
                at = (last + p) * LANES
                halo_send[(3 + c) * per + p:(3 + c) * per + p + 1] = obs_ref[
                    c:c + 1, at:at + LANES]
        halo_send[5 * per:] = jnp.zeros((halo_send.shape[0] - 5 * per, LANES), F32)
        pl.semaphore_wait(barrier, len(greeted))
        halo_copy = copy(halo_send, halo, 0, after)

    degree = har_ref[0:1, :].astype(F32)
    order = har_ref[1:2, :]
    size = jnp.abs(order).astype(F32)
    phase = jnp.where(order >= 0, 0.0, -0.25).astype(F32)
    turned[...] = jnp.zeros((LANES, LANES), F32)
    number = 0
    for values in (degree, size, phase):
        for t in range(col_tiles):
            turned[number:number + 1, :] = values[:, t * LANES:(t + 1) * LANES]
            number += 1
    columns = turned[...].T
    for number in range(3):
        for t in range(col_tiles):
            waves[number, t * LANES:(t + 1) * LANES, :] = spread(columns, number * col_tiles + t)

    below = lax.broadcasted_iota(jnp.int32, (EXTRA, LANES), 0) == 0

    def design_block(slot):
        for half in range(per):
            tile = slot * per + half
            lanes = slice(half * LANES, (half + 1) * LANES)
            theta_high, theta_low = turns(col_ref[pl.ds(tile, 1), :])
            phi_high, phi_low = turns(lon_ref[pl.ds(tile, 1), :])
            for chunk in range(width // CHUNK):
                rows = slice(chunk * CHUNK, (chunk + 1) * CHUNK)
                n = waves[0, rows, :]
                m = waves[1, rows, :]
                a = n * theta_high
                a = (a - nearest(a)) + n * theta_low
                b = m * phi_high + waves[2, rows, :]
                b = (b - nearest(b)) + m * phi_low
                ua = a * a
                ub = b * b
                sin_a = a * poly(ua, SIN_C)
                cos_a = poly(ua, COS_C)
                sin_b = b * poly(ub, SIN_C)
                w = 1.0 - sin_b * sin_b
                fresh[0, rows, lanes] = ((1.0 - sin_a * sin_a) * w).astype(BF16)
                fresh[1, rows, lanes] = ((sin_a * cos_a) * w).astype(BF16)
            at = pl.multiple_of(tile * LANES, LANES)
            for c in range(2):
                values = obs_ref[c:c + 1, pl.ds(at, LANES)]
                fresh[c, width:, lanes] = jnp.where(
                    below, jnp.broadcast_to(values, (EXTRA, LANES)), 0.0
                ).astype(BF16)

    def shift():
        window[:, :, taps_n:] = window[:, :, :taps_n]
        window[:, :, :taps_n] = fresh[...]

    window[:, :, :taps_n] = jnp.zeros((2, width + EXTRA, taps_n), BF16)

    @pl.loop(0, 2)
    def _(step):
        design_block(blocks - 1 - step)
        shift()

    j = lax.broadcasted_iota(jnp.int32, (taps_n, taps_n), 0)
    i = lax.broadcasted_iota(jnp.int32, (taps_n, taps_n), 1)
    for c in range(2):
        row = jnp.broadcast_to(taps_ref[c:c + 1, :].astype(F32), (8, taps_n))
        base = pltpu.roll(row, 0, 1, stride=1, stride_axis=0)
        for r in range(0, taps_n, 8):
            around = pltpu.roll(base, r, 1) if r else base
            early = i[r:r + 8] < j[r:r + 8]
            table[c, r:r + 8, :] = jnp.where(early, around, 0.0)
            table[c, taps_n + r:taps_n + r + 8, :] = jnp.where(early, 0.0, around)

    first_lane = lax.broadcasted_iota(jnp.int32, (LANES, LANES), 0)
    second_lane = lax.broadcasted_iota(jnp.int32, (LANES, LANES), 1)
    ones = jnp.ones((LANES, LANES), BF16)

    def counted(flags, lanes, rows):
        here = jnp.dot(flags, lanes.astype(BF16), preferred_element_type=F32)
        others = jnp.dot(rows.astype(BF16), flags, preferred_element_type=F32)
        return here + jnp.dot(others.astype(BF16), ones, preferred_element_type=F32)

    first_row = lax.broadcasted_iota(jnp.int32, (own, own), 0)
    second_row = lax.broadcasted_iota(jnp.int32, (own, own), 1)
    lab[0:own] = counted(
        seg_ref[...].astype(F32).astype(BF16), first_lane <= second_lane, second_row < first_row
    )
    if fused:
        halo_copy.wait()
    first_row = lax.broadcasted_iota(jnp.int32, (halo.shape[0], halo.shape[0]), 0)
    second_row = lax.broadcasted_iota(jnp.int32, (halo.shape[0], halo.shape[0]), 1)
    later = (first_row < second_row) & (second_row < 3 * per)
    ahead = counted(halo[...].astype(BF16), first_lane > second_lane, later)
    first = row_index == 0
    lab[own:own + per] = jnp.where(first, -1.0, -ahead[2 * per:3 * per])
    for r in range(per):
        for c in range(2):
            at = (3 + c) * per + r
            obs_ref[c:c + 1, (own + r) * LANES:(own + r + 1) * LANES] = halo[at:at + 1]
    col_ref[own:own + per] = halo[0:per]
    lon_ref[own:own + per] = halo[per:2 * per]
    turned[0:own + per] = lab[...]
    columns = turned[...].T
    for tile in range(own + per):
        lab_col[tile * LANES:(tile + 1) * LANES, :] = spread(columns, tile)

    half_width = width // 2
    half_tiles = half_width // LANES
    gram[...] = jnp.zeros(gram.shape, F32)

    def filter_block(block):
        slots = (lax.rem(block + blocks, blocks + 1), block)
        for half in range(per):
            lanes = slice(half * LANES, (half + 1) * LANES)
            out_label = lab[pl.ds(block * per + half, 1), :]
            for part in range(2 * per):
                at = slice(part * LANES, (part + 1) * LANES)
                tile = slots[part // per] * per + part % per
                got = lab_col[pl.ds(pl.multiple_of(tile * LANES, LANES), LANES), :]
                same = got == out_label
                for c in range(2):
                    matrix[c, at, lanes] = jnp.where(same, table[c, at, lanes], 0.0).astype(BF16)
        for c in range(2):
            filt[:, c * taps_n:(c + 1) * taps_n] = jnp.dot(
                window[c], matrix[c], preferred_element_type=F32
            ).astype(BF16)

    def gram_half(half):
        from_row = half * half_width
        part = lax.dot_general(
            filt[from_row:, :], filt[from_row:from_row + half_width, :],
            (((1,), (1,)), ((), ())), preferred_element_type=F32,
        )
        for t in range(half_tiles):
            gram[half * half_tiles + t, from_row:, :] += part[:, t * LANES:(t + 1) * LANES]

    @pl.loop(0, blocks - 1)
    def _(step):
        block = blocks - 1 - step
        design_block(lax.rem(block - 2 + blocks + 1, blocks + 1))
        filter_block(block)
        gram_half(0)
        gram_half(1)
        shift()

    filter_block(0)
    copies_a = []
    for half in range(2):
        gram_half(half)
        if half == 1:
            for t in range(half_tiles):
                for q in range(half_tiles):
                    gram[half_tiles + t, q * LANES:(q + 1) * LANES, :] = gram[
                        q, half_width + t * LANES:half_width + (t + 1) * LANES, :].T
        if fused:
            tile_rows = width // n_row
            for t in range(half * half_tiles, (half + 1) * half_tiles):
                for zz in range(n_z):
                    at = pl.multiple_of((2 * zz + 1 - core) * tile_rows, tile_rows)
                    sa[t, zz] = gram[t, pl.ds(at, tile_rows), :].astype(BF16)
            part = pl.ds(half * half_tiles, half_tiles)
            copies_a.append(copy(sa.at[part], ra.at[part], 1 + half, twin))

    eye = lax.broadcasted_iota(jnp.int32, (LANES, LANES), 0) == lax.broadcasted_iota(
        jnp.int32, (LANES, LANES), 1
    )
    small = []
    for t in range(col_tiles):
        small.append(gram[t, width:width + 1, :])
    for t in range(col_tiles):
        square = gram[t, t * LANES:(t + 1) * LANES, :]
        small.append(jnp.sum(jnp.where(eye, square, 0.0), axis=0, keepdims=True))
    if not fused:
        for r, row in enumerate(small):
            small_ref[r:r + 1, :] = row
        return

    for r, row in enumerate(small):
        rs[0, r:r + 1, :] = row
    small_a = copy(rs.at[0], rr.at[0], 3, twin)
    for c in copies_a:
        c.wait()
    for t in range(col_tiles):
        for zz in range(n_z):
            at = pl.multiple_of((2 * zz + core) * tile_rows, tile_rows)
            gram[t, pl.ds(zz * tile_rows, tile_rows), :] = gram[
                t, pl.ds(at, tile_rows), :] + ra[t, zz].astype(F32)

    def held(t, zz):
        return gram[t, pl.ds(pl.multiple_of(zz * tile_rows, tile_rows), tile_rows), :]

    def add(t, zz, values):
        at = pl.ds(pl.multiple_of(zz * tile_rows, tile_rows), tile_rows)
        gram[t, at, :] = gram[t, at, :] + values.astype(F32)

    z_half = n_z // 2
    for k in range(2):
        for q in range(z_half):
            sb[0, k, q] = held(2 * (1 - y) + k, q).astype(BF16)
            sb[1, k, q] = held(2 * k + 1 - x, z_half + q).astype(BF16)
    copies_b = [copy(sb.at[0], rb.at[0], 4, y_peer), copy(sb.at[1], rb.at[1], 5, x_peer)]
    small_a.wait()
    rs[1] = rs[0] + rr[0]
    small_b = copy(rs.at[1], rr.at[1], 6, y_peer)
    copies_b[0].wait()
    for q in range(z_half):
        sc[0, q] = (held(2 * y + 1 - x, q) + rb[0, 1 - x, q].astype(F32)).astype(BF16)
    copies_c = [copy(sc.at[0], rc.at[0], 7, x_peer)]
    copies_b[1].wait()
    for q in range(z_half):
        sc[1, q] = (held(2 * (1 - y) + x, z_half + q) + rb[1, 1 - y, q].astype(F32)).astype(BF16)
    copies_c.append(copy(sc.at[1], rc.at[1], 8, y_peer))
    for q in range(z_half):
        add(grp_index, q, rb[0, x, q])
        add(grp_index, z_half + q, rb[1, y, q])
    small_b.wait()
    rs[2] = rs[1] + rr[1]
    small_c = copy(rs.at[2], rr.at[2], 9, x_peer)
    for s in range(2):
        copies_c[s].wait()
        for q in range(z_half):
            add(grp_index, s * z_half + q, rc[s, q])
    copies_d = []
    for k in range(1, n_z):
        sd[k - 1] = held(grp_index, lax.rem(z + k, n_z)).astype(BF16)
        copies_d.append(copy(sd.at[k - 1], rd.at[k - 1], 9 + k, z_peers[k - 1]))
    small_c.wait()
    rz[z] = rs[2] + rr[2]
    small_d = []
    for k in range(1, n_z):
        small_d.append(copy(rz.at[z], rz.at[z], 8 + n_z + k, z_peers[k - 1]))
    total = held(grp_index, z)
    for k in range(1, n_z):
        copies_d[k - 1].wait()
        total = total + rd[k - 1].astype(F32)
    row_at = row_index * tile_rows + lax.broadcasted_iota(jnp.int32, total.shape, 0)
    col_at = grp_index * LANES + lax.broadcasted_iota(jnp.int32, total.shape, 1)
    out_ref[...] = jnp.where(row_at == col_at, 0.0, total * gram_scale)
    for c in small_d:
        c.wait()
    total = rz[0]
    for zz in range(1, n_z):
        total = total + rz[zz]
    small_ref[0:col_tiles] = total[0:col_tiles] * gram_scale
    small_ref[col_tiles:] = total[col_tiles:] * row_scale


def on_device(colatitude, longitude, observed, filter_taps, segment_start, harmonic):
    rows_here = colatitude.shape[0]
    taps_n = filter_taps.shape[1]
    width = harmonic.shape[1]
    n_grp = lax.axis_size("grp")
    n_row = lax.axis_size("row")
    blocks = rows_here // taps_n
    per = taps_n // LANES
    tiles = width // LANES
    rows_total = rows_here * n_grp * n_row
    row_scale = 1.0 / rows_total
    gram_scale = 1.0 / math.sqrt(rows_total)
    fused = FUSED and n_grp == 4 and n_row == 8 and width == n_grp * LANES
    split = [a.reshape(rows_here // LANES, LANES) for a in (colatitude, longitude, segment_start)]
    inputs = [split[0], split[1], observed, filter_taps, split[2], harmonic]
    window = rows_here + taps_n
    scratch = [
        pltpu.VMEM((window // LANES, LANES), F32),
        pltpu.VMEM((window // LANES, LANES), F32),
        pltpu.VMEM(observed.shape, observed.dtype),
        pltpu.VMEM(filter_taps.shape, filter_taps.dtype),
        pltpu.VMEM((rows_here // LANES, LANES), segment_start.dtype),
        pltpu.VMEM(harmonic.shape, harmonic.dtype),
        pltpu.SemaphoreType.DMA((6,)),
        pltpu.VMEM((2, window), F32),
        pltpu.VMEM((2, width + EXTRA, taps_n), BF16),
        pltpu.VMEM((2, width + EXTRA, 2 * taps_n), BF16),
        pltpu.VMEM((width + EXTRA, 2 * taps_n), BF16),
        pltpu.VMEM((2, 2 * taps_n, taps_n), F32),
        pltpu.VMEM((2, 2 * taps_n, taps_n), BF16),
        pltpu.VMEM((window, LANES), F32),
        pltpu.VMEM((window // LANES, LANES), F32),
        pltpu.VMEM((3, width, LANES), F32),
        pltpu.VMEM((LANES, LANES), F32),
    ]
    gram_shape = (tiles, width + EXTRA, LANES)
    small_shape = jax.ShapeDtypeStruct((2 * tiles, LANES), F32)
    halo_shape = (8 * per, LANES)
    if fused:
        tile_rows = width // n_row
        n_z = n_row // 2
        tile = (tile_rows, LANES)
        copies = 9 + 2 * n_z
        scratch += [
            pltpu.VMEM(gram_shape, F32),
            pltpu.VMEM(halo_shape, F32),
            pltpu.VMEM(halo_shape, F32),
            pltpu.VMEM((tiles, n_z) + tile, BF16),
            pltpu.VMEM((tiles, n_z) + tile, BF16),
            pltpu.VMEM((2, 2, n_z // 2) + tile, BF16),
            pltpu.VMEM((2, 2, n_z // 2) + tile, BF16),
            pltpu.VMEM((2, n_z // 2) + tile, BF16),
            pltpu.VMEM((2, n_z // 2) + tile, BF16),
            pltpu.VMEM((n_z - 1,) + tile, BF16),
            pltpu.VMEM((n_z - 1,) + tile, BF16),
            pltpu.VMEM((3, 2 * tiles, LANES), F32),
            pltpu.VMEM((3, 2 * tiles, LANES), F32),
            pltpu.VMEM((n_z, 2 * tiles, LANES), F32),
            pltpu.SemaphoreType.DMA((copies,)),
            pltpu.SemaphoreType.DMA((copies,)),
        ]
        main_shape = jax.ShapeDtypeStruct((tile_rows, LANES), F32)
    else:
        last = rows_here // LANES - per
        pieces = [split[0][last:], split[1][last:], split[2][last:].astype(F32)]
        pieces.append(observed[:, rows_here - taps_n:].astype(F32).reshape(2 * per, LANES))
        pieces.append(jnp.zeros((3 * per, LANES), F32))
        pairs = [(k, k + 1) for k in range(n_row - 1)]
        inputs.append(lax.ppermute(jnp.concatenate(pieces), "row", pairs))
        main_shape = jax.ShapeDtypeStruct(gram_shape, F32)
    params = dict(vmem_limit_bytes=64 * 1024 * 1024)
    if fused:
        params.update(collective_id=0, has_side_effects=True)
    main, small = pl.pallas_call(
        functools.partial(
            local_kernel, fused, n_grp, n_row, blocks, taps_n, width, gram_scale, row_scale
        ),
        out_shape=(main_shape, small_shape),
        in_specs=[pl.BlockSpec(memory_space=pltpu.HBM)] * 6
        + [pl.BlockSpec(memory_space=pltpu.VMEM)] * (len(inputs) - 6),
        out_specs=(pl.BlockSpec(memory_space=pltpu.VMEM),) * 2,
        scratch_shapes=scratch,
        compiler_params=pltpu.CompilerParams(**params),
        name="normal_equations",
    )(*inputs)
    if fused:
        return (main, small[:tiles].reshape(width), small[tiles:].reshape(width))
    gram = main[:, :width].transpose(1, 0, 2).reshape(width, width)
    owned = lax.psum_scatter(gram, "row", scatter_dimension=0, tiled=True)
    normal = lax.psum_scatter(owned, "grp", scatter_dimension=1, tiled=True)
    small = lax.psum(small, ("grp", "row"))
    row_at = lax.axis_index("row") * normal.shape[0] + lax.broadcasted_iota(
        jnp.int32, normal.shape, 0
    )
    col_at = lax.axis_index("grp") * normal.shape[1] + lax.broadcasted_iota(
        jnp.int32, normal.shape, 1
    )
    normal = jnp.where(row_at == col_at, 0.0, normal * gram_scale)
    right_side = small[:tiles].reshape(width) * gram_scale
    diagonal = small[tiles:].reshape(width) * row_scale
    return (normal, right_side, diagonal)


def solution(mesh):
    placed = (
        P(("grp", "row")),
        P(("grp", "row")),
        P(None, ("grp", "row")),
        P(),
        P(("grp", "row")),
        P(),
    )
    return jax.shard_map(
        on_device,
        mesh=mesh,
        in_specs=placed,
        out_specs=(P("row", "grp"), P(), P()),
        check_vma=False,
    )
```

```python
import functools
import math

import jax
import jax.numpy as jnp
from jax import lax
from jax.experimental import pallas as pl
from jax.experimental.pallas import tpu as pltpu
from jax.sharding import PartitionSpec as P

F32 = jnp.float32
BF16 = jnp.bfloat16
LANES = 128
EXTRA = 16
CHUNK = 64
SIN_C = (4.442866325378418, -7.307384967803955, 3.594230890274048, -0.7829042077064514)
COS_C = (1.41420316696167, -6.977553367614746, 5.714066982269287, -1.7246402502059937)
TURN_HIGH = 2608.0 / 16384.0
TURN_LOW = 1.0 / (2.0 * math.pi) - TURN_HIGH
TURN_UNIT = 2.0**-32
FUSED = True


def poly(u, coefficients):
    total = coefficients[-1]
    for c in coefficients[-2::-1]:
        total = total * u + c
    return total


def nearest(x):
    return (x + 12582912.0) - 12582912.0


def spread(columns, k):
    return jnp.broadcast_to(columns[:, k:k + 1], (LANES, LANES))


def turns(angle):
    head = nearest(angle * 1024.0) * (1.0 / 1024.0)
    tail = angle - head
    coarse = head * TURN_HIGH
    high = nearest(coarse * 32768.0)
    low = (coarse - high * (1.0 / 32768.0)) + (head * TURN_LOW + tail * (TURN_HIGH + TURN_LOW))
    fine = nearest(low * 2.0**32)
    return high.astype(jnp.int32) * 131072 + fine.astype(jnp.int32)


def hand_on_kernel(*refs):
    count = (len(refs) - 1) // 2
    copies = [
        pltpu.make_async_copy(refs[k], refs[count + k], refs[-1].at[k]) for k in range(count)
    ]
    for c in copies:
        c.start()
    for c in copies:
        c.wait()


def local_kernel(
    fused, n_grp, n_row, blocks, taps_n, width, gram_scale, row_scale,
    col_in, lon_in, obs_in, taps_in, seg_in, har_in, *refs,
):
    if fused:
        (out_ref, right_ref, diag_ref, col_ref, lon_ref, obs_got, taps_ref, seg_ref, har_ref, in_sem,
         obs_ref, fresh, window, filt, table, matrix, lab_col, lab, waves, turned, gram,
         halo_send, halo, sa, ra, sb, rb, sc, rc, sd, rd, rs, rr, rz, send_sem, recv_sem) = refs
    else:
        (halo, gram, small_ref, col_ref, lon_ref, obs_got, taps_ref, seg_ref, har_ref, in_sem,
         obs_ref, fresh, window, filt, table, matrix, lab_col, lab, waves, turned) = refs
    per = taps_n // LANES
    own = blocks * per
    col_tiles = width // LANES
    row_index = lax.axis_index("row")
    grp_index = lax.axis_index("grp")

    fetched = (
        (har_in, har_ref), (taps_in, taps_ref), (col_in, col_ref.at[0:own]),
        (lon_in, lon_ref.at[0:own]), (seg_in, seg_ref), (obs_in, obs_got),
    )
    fetches = [
        pltpu.make_async_copy(src, dst, in_sem.at[k]) for k, (src, dst) in enumerate(fetched)
    ]
    for fetch in fetches:
        fetch.start()

    if fused:
        core = lax.rem(row_index, 2)
        z = row_index // 2
        y = grp_index // 2
        x = lax.rem(grp_index, 2)
        n_z = n_row // 2
        twin = (grp_index, row_index + 1 - 2 * core)
        y_peer = (lax.rem(grp_index + 2, 4), row_index)
        x_peer = (grp_index + 1 - 2 * x, row_index)
        z_peers = [(grp_index, lax.rem(row_index + 2 * k, n_row)) for k in range(1, n_z)]
        after = (grp_index, lax.rem(row_index + 1, n_row))
        before = (grp_index, lax.rem(row_index + n_row - 1, n_row))
        greeted = [twin, y_peer, x_peer, after, before] + z_peers
        barrier = pltpu.get_barrier_semaphore()
        for peer in greeted:
            pl.semaphore_signal(barrier, inc=1, device_id=peer, device_id_type=pl.DeviceIdType.MESH)

        def copy(src, dst, number, peer):
            c = pltpu.make_async_remote_copy(
                src_ref=src, dst_ref=dst,
                send_sem=send_sem.at[number], recv_sem=recv_sem.at[number],
                device_id=peer, device_id_type=pl.DeviceIdType.MESH,
            )
            c.start()
            return c

    for fetch in fetches:
        fetch.wait()
    obs_ref[:, 0:own * LANES] = obs_got[...].astype(F32)

    if fused:
        last = own - per
        halo_send[0:per] = col_ref[last:last + per]
        halo_send[per:2 * per] = lon_ref[last:last + per]
        halo_send[2 * per:3 * per] = seg_ref[last:last + per].astype(F32)
        for c in range(2):
            for p in range(per):
                at = (last + p) * LANES
                halo_send[(3 + c) * per + p:(3 + c) * per + p + 1] = obs_ref[
                    c:c + 1, at:at + LANES]
        halo_send[5 * per:] = jnp.zeros((halo_send.shape[0] - 5 * per, LANES), F32)

    degree = har_ref[0:1, :].astype(F32)
    order = har_ref[1:2, :]
    size = jnp.abs(order).astype(F32)
    phase = jnp.where(order >= 0, 0.0, -1.0).astype(F32)
    turned[...] = jnp.zeros((LANES, LANES), F32)
    number = 0
    for values in (degree, size, phase):
        for t in range(col_tiles):
            turned[number:number + 1, :] = values[:, t * LANES:(t + 1) * LANES]
            number += 1
    columns = turned[...].T
    for number in range(3):
        for t in range(col_tiles):
            unit = 1 << 30 if number == 2 else 1
            waves[number, t * LANES:(t + 1) * LANES, :] = (
                spread(columns, number * col_tiles + t).astype(jnp.int32) * unit
            )

    below = lax.broadcasted_iota(jnp.int32, (EXTRA, LANES), 0) == 0

    def design_block(slot):
        for half in range(per):
            tile = slot * per + half
            lanes = slice(half * LANES, (half + 1) * LANES)
            theta = turns(col_ref[pl.ds(tile, 1), :])
            phi = turns(lon_ref[pl.ds(tile, 1), :])
            for chunk in range(width // CHUNK):
                rows = slice(chunk * CHUNK, (chunk + 1) * CHUNK)
                a = (waves[0, rows, :] * theta).astype(F32) * TURN_UNIT
                b = (waves[1, rows, :] * phi + waves[2, rows, :]).astype(F32) * TURN_UNIT
                ua = a * a
                ub = b * b
                sin_a = a * poly(ua, SIN_C)
                cos_a = poly(ua, COS_C)
                sin_b = b * poly(ub, SIN_C)
                w = 1.0 - sin_b * sin_b
                sin_w = sin_a * w
                fresh[0, rows, lanes] = (w - sin_a * sin_w).astype(BF16)
                fresh[1, rows, lanes] = (cos_a * sin_w).astype(BF16)
            at = pl.multiple_of(tile * LANES, LANES)
            for c in range(2):
                values = obs_ref[c:c + 1, pl.ds(at, LANES)]
                fresh[c, width:, lanes] = jnp.where(
                    below, jnp.broadcast_to(values, (EXTRA, LANES)), 0.0
                ).astype(BF16)

    def shift():
        window[:, :, taps_n:] = window[:, :, :taps_n]
        window[:, :, :taps_n] = fresh[...]

    window[:, :, :taps_n] = jnp.zeros((2, width + EXTRA, taps_n), BF16)

    @pl.loop(0, 2)
    def _(step):
        design_block(blocks - 1 - step)
        shift()

    if fused:
        pl.semaphore_wait(barrier, len(greeted))
        halo_copy = copy(halo_send, halo, 0, after)

    j = lax.broadcasted_iota(jnp.int32, (taps_n, taps_n), 0)
    i = lax.broadcasted_iota(jnp.int32, (taps_n, taps_n), 1)
    for c in range(2):
        row = jnp.broadcast_to(taps_ref[c:c + 1, :].astype(F32), (8, taps_n))
        base = pltpu.roll(row, 0, 1, stride=1, stride_axis=0)
        for r in range(0, taps_n, 8):
            around = pltpu.roll(base, r, 1) if r else base
            early = i[r:r + 8] < j[r:r + 8]
            table[c, r:r + 8, :] = jnp.where(early, around, 0.0)
            table[c, taps_n + r:taps_n + r + 8, :] = jnp.where(early, 0.0, around)

    first_lane = lax.broadcasted_iota(jnp.int32, (LANES, LANES), 0)
    second_lane = lax.broadcasted_iota(jnp.int32, (LANES, LANES), 1)
    ones = jnp.ones((LANES, LANES), BF16)

    def counted(flags, lanes, rows):
        here = jnp.dot(flags, lanes.astype(BF16), preferred_element_type=F32)
        others = jnp.dot(rows.astype(BF16), flags, preferred_element_type=F32)
        return here + jnp.dot(others.astype(BF16), ones, preferred_element_type=F32)

    first_row = lax.broadcasted_iota(jnp.int32, (own, own), 0)
    second_row = lax.broadcasted_iota(jnp.int32, (own, own), 1)
    lab[0:own] = counted(
        seg_ref[...].astype(F32).astype(BF16), first_lane <= second_lane, second_row < first_row
    )
    if fused:
        halo_copy.wait()
    first_row = lax.broadcasted_iota(jnp.int32, (halo.shape[0], halo.shape[0]), 0)
    second_row = lax.broadcasted_iota(jnp.int32, (halo.shape[0], halo.shape[0]), 1)
    later = (first_row < second_row) & (second_row < 3 * per)
    ahead = counted(halo[...].astype(BF16), first_lane > second_lane, later)
    first = row_index == 0
    lab[own:own + per] = jnp.where(first, -1.0, -ahead[2 * per:3 * per])
    for r in range(per):
        for c in range(2):
            at = (3 + c) * per + r
            obs_ref[c:c + 1, (own + r) * LANES:(own + r + 1) * LANES] = halo[at:at + 1]
    col_ref[own:own + per] = halo[0:per]
    lon_ref[own:own + per] = halo[per:2 * per]
    turned[0:own + per] = lab[...]
    columns = turned[...].T
    for tile in range(own + per):
        lab_col[tile * LANES:(tile + 1) * LANES, :] = spread(columns, tile)

    half_width = width // 2
    half_tiles = half_width // LANES
    gram[...] = jnp.zeros(gram.shape, F32)

    def filter_block(block):
        slots = (lax.rem(block + blocks, blocks + 1), block)
        for half in range(per):
            lanes = slice(half * LANES, (half + 1) * LANES)
            out_label = lab[pl.ds(block * per + half, 1), :]
            for part in range(2 * per):
                at = slice(part * LANES, (part + 1) * LANES)
                tile = slots[part // per] * per + part % per
                got = lab_col[pl.ds(pl.multiple_of(tile * LANES, LANES), LANES), :]
                same = got == out_label
                for c in range(2):
                    matrix[c, at, lanes] = jnp.where(same, table[c, at, lanes], 0.0).astype(BF16)
        for c in range(2):
            filt[:, c * taps_n:(c + 1) * taps_n] = jnp.dot(
                window[c], matrix[c], preferred_element_type=F32
            ).astype(BF16)

    def gram_half(half):
        from_row = half * half_width
        part = lax.dot_general(
            filt[from_row:, :], filt[from_row:from_row + half_width, :],
            (((1,), (1,)), ((), ())), preferred_element_type=F32,
        )
        for t in range(half_tiles):
            gram[half * half_tiles + t, from_row:, :] += part[:, t * LANES:(t + 1) * LANES]

    @pl.loop(0, blocks - 1)
    def _(step):
        block = blocks - 1 - step
        design_block(lax.rem(block - 2 + blocks + 1, blocks + 1))
        filter_block(block)
        gram_half(0)
        gram_half(1)
        shift()

    filter_block(0)
    copies_a = []
    for half in range(2):
        gram_half(half)
        if half == 1:
            for t in range(half_tiles):
                for q in range(half_tiles):
                    gram[half_tiles + t, q * LANES:(q + 1) * LANES, :] = gram[
                        q, half_width + t * LANES:half_width + (t + 1) * LANES, :].T
        if fused:
            tile_rows = width // n_row
            for t in range(half * half_tiles, (half + 1) * half_tiles):
                for zz in range(n_z):
                    at = pl.multiple_of((2 * zz + 1 - core) * tile_rows, tile_rows)
                    sa[t, zz] = gram[t, pl.ds(at, tile_rows), :].astype(BF16)
            part = pl.ds(half * half_tiles, half_tiles)
            copies_a.append(copy(sa.at[part], ra.at[part], 1 + half, twin))

    eye = lax.broadcasted_iota(jnp.int32, (LANES, LANES), 0) == lax.broadcasted_iota(
        jnp.int32, (LANES, LANES), 1
    )
    small = []
    for t in range(col_tiles):
        small.append(gram[t, width:width + 1, :])
    for t in range(col_tiles):
        square = gram[t, t * LANES:(t + 1) * LANES, :]
        small.append(jnp.sum(jnp.where(eye, square, 0.0), axis=0, keepdims=True))
    if not fused:
        for r, row in enumerate(small):
            small_ref[r:r + 1, :] = row
        return

    for r, row in enumerate(small):
        rs[0, r:r + 1, :] = row
    small_a = copy(rs.at[0], rr.at[0], 3, twin)
    for c in copies_a:
        c.wait()
    for t in range(col_tiles):
        for zz in range(n_z):
            at = pl.multiple_of((2 * zz + core) * tile_rows, tile_rows)
            gram[t, pl.ds(zz * tile_rows, tile_rows), :] = gram[
                t, pl.ds(at, tile_rows), :] + ra[t, zz].astype(F32)

    def held(t, zz):
        return gram[t, pl.ds(pl.multiple_of(zz * tile_rows, tile_rows), tile_rows), :]

    def add(t, zz, values):
        at = pl.ds(pl.multiple_of(zz * tile_rows, tile_rows), tile_rows)
        gram[t, at, :] = gram[t, at, :] + values.astype(F32)

    z_half = n_z // 2
    for k in range(2):
        for q in range(z_half):
            sb[0, k, q] = held(2 * (1 - y) + k, q).astype(BF16)
            sb[1, k, q] = held(2 * k + 1 - x, z_half + q).astype(BF16)
    copies_b = [copy(sb.at[0], rb.at[0], 4, y_peer), copy(sb.at[1], rb.at[1], 5, x_peer)]
    small_a.wait()
    rs[1] = rs[0] + rr[0]
    small_b = copy(rs.at[1], rr.at[1], 6, y_peer)
    copies_b[0].wait()
    for q in range(z_half):
        sc[0, q] = (held(2 * y + 1 - x, q) + rb[0, 1 - x, q].astype(F32)).astype(BF16)
    copies_c = [copy(sc.at[0], rc.at[0], 7, x_peer)]
    copies_b[1].wait()
    for q in range(z_half):
        sc[1, q] = (held(2 * (1 - y) + x, z_half + q) + rb[1, 1 - y, q].astype(F32)).astype(BF16)
    copies_c.append(copy(sc.at[1], rc.at[1], 8, y_peer))
    for q in range(z_half):
        add(grp_index, q, rb[0, x, q])
        add(grp_index, z_half + q, rb[1, y, q])
    small_b.wait()
    rs[2] = rs[1] + rr[1]
    small_c = copy(rs.at[2], rr.at[2], 9, x_peer)
    for s in range(2):
        copies_c[s].wait()
        for q in range(z_half):
            add(grp_index, s * z_half + q, rc[s, q])
    copies_d = []
    for k in range(1, n_z):
        sd[k - 1] = held(grp_index, lax.rem(z + k, n_z)).astype(BF16)
        copies_d.append(copy(sd.at[k - 1], rd.at[k - 1], 9 + k, z_peers[k - 1]))
    small_c.wait()
    rz[z] = rs[2] + rr[2]
    small_d = []
    for k in range(1, n_z):
        small_d.append(copy(rz.at[z], rz.at[z], 8 + n_z + k, z_peers[k - 1]))
    total = held(grp_index, z)
    for k in range(1, n_z):
        copies_d[k - 1].wait()
        total = total + rd[k - 1].astype(F32)
    row_at = row_index * tile_rows + lax.broadcasted_iota(jnp.int32, total.shape, 0)
    col_at = grp_index * LANES + lax.broadcasted_iota(jnp.int32, total.shape, 1)
    out_ref[...] = jnp.where(row_at == col_at, 0.0, total * gram_scale)
    for c in small_d:
        c.wait()
    total = rz[0]
    for zz in range(1, n_z):
        total = total + rz[zz]
    right_ref[...] = total[0:col_tiles] * gram_scale
    diag_ref[...] = total[col_tiles:] * row_scale


def on_device(colatitude, longitude, observed, filter_taps, segment_start, harmonic):
    rows_here = colatitude.shape[0]
    taps_n = filter_taps.shape[1]
    width = harmonic.shape[1]
    n_grp = lax.axis_size("grp")
    n_row = lax.axis_size("row")
    blocks = rows_here // taps_n
    per = taps_n // LANES
    tiles = width // LANES
    rows_total = rows_here * n_grp * n_row
    row_scale = 1.0 / rows_total
    gram_scale = 1.0 / math.sqrt(rows_total)
    fused = FUSED and n_grp == 4 and n_row == 8 and width == n_grp * LANES
    split = [a.reshape(rows_here // LANES, LANES) for a in (colatitude, longitude, segment_start)]
    inputs = [split[0], split[1], observed, filter_taps, split[2], harmonic]
    window = rows_here + taps_n
    scratch = [
        pltpu.VMEM((window // LANES, LANES), F32),
        pltpu.VMEM((window // LANES, LANES), F32),
        pltpu.VMEM(observed.shape, observed.dtype),
        pltpu.VMEM(filter_taps.shape, filter_taps.dtype),
        pltpu.VMEM((rows_here // LANES, LANES), segment_start.dtype),
        pltpu.VMEM(harmonic.shape, harmonic.dtype),
        pltpu.SemaphoreType.DMA((6,)),
        pltpu.VMEM((2, window), F32),
        pltpu.VMEM((2, width + EXTRA, taps_n), BF16),
        pltpu.VMEM((2, width + EXTRA, 2 * taps_n), BF16),
        pltpu.VMEM((width + EXTRA, 2 * taps_n), BF16),
        pltpu.VMEM((2, 2 * taps_n, taps_n), F32),
        pltpu.VMEM((2, 2 * taps_n, taps_n), BF16),
        pltpu.VMEM((window, LANES), F32),
        pltpu.VMEM((window // LANES, LANES), F32),
        pltpu.VMEM((3, width, LANES), jnp.int32),
        pltpu.VMEM((LANES, LANES), F32),
    ]
    gram_shape = (tiles, width + EXTRA, LANES)
    small_shapes = (jax.ShapeDtypeStruct((2 * tiles, LANES), F32),)
    halo_shape = (8 * per, LANES)
    if fused:
        tile_rows = width // n_row
        n_z = n_row // 2
        tile = (tile_rows, LANES)
        copies = 9 + 2 * n_z
        scratch += [
            pltpu.VMEM(gram_shape, F32),
            pltpu.VMEM(halo_shape, F32),
            pltpu.VMEM(halo_shape, F32),
            pltpu.VMEM((tiles, n_z) + tile, BF16),
            pltpu.VMEM((tiles, n_z) + tile, BF16),
            pltpu.VMEM((2, 2, n_z // 2) + tile, BF16),
            pltpu.VMEM((2, 2, n_z // 2) + tile, BF16),
            pltpu.VMEM((2, n_z // 2) + tile, BF16),
            pltpu.VMEM((2, n_z // 2) + tile, BF16),
            pltpu.VMEM((n_z - 1,) + tile, BF16),
            pltpu.VMEM((n_z - 1,) + tile, BF16),
            pltpu.VMEM((3, 2 * tiles, LANES), F32),
            pltpu.VMEM((3, 2 * tiles, LANES), F32),
            pltpu.VMEM((n_z, 2 * tiles, LANES), F32),
            pltpu.SemaphoreType.DMA((copies,)),
            pltpu.SemaphoreType.DMA((copies,)),
        ]
        main_shape = jax.ShapeDtypeStruct((tile_rows, LANES), F32)
        small_shapes = (jax.ShapeDtypeStruct((tiles, LANES), F32),) * 2
    else:
        last = rows_here // LANES - per
        pieces = [split[0][last:], split[1][last:], split[2][last:].astype(F32)]
        pieces.append(observed[:, rows_here - taps_n:].astype(F32).reshape(2 * per, LANES))
        pieces.append(jnp.zeros((3 * per, LANES), F32))
        pairs = [(k, k + 1) for k in range(n_row - 1)]
        inputs.append(lax.ppermute(jnp.concatenate(pieces), "row", pairs))
        main_shape = jax.ShapeDtypeStruct(gram_shape, F32)
    params = dict(vmem_limit_bytes=64 * 1024 * 1024)
    if fused:
        params.update(collective_id=0, has_side_effects=True)
    main, *small = pl.pallas_call(
        functools.partial(
            local_kernel, fused, n_grp, n_row, blocks, taps_n, width, gram_scale, row_scale
        ),
        out_shape=(main_shape,) + small_shapes,
        in_specs=[pl.BlockSpec(memory_space=pltpu.HBM)] * 6
        + [pl.BlockSpec(memory_space=pltpu.VMEM)] * (len(inputs) - 6),
        out_specs=(pl.BlockSpec(memory_space=pltpu.VMEM),) * (1 + len(small_shapes)),
        scratch_shapes=scratch,
        compiler_params=pltpu.CompilerParams(**params),
        name="normal_equations",
    )(*inputs)
    if fused:
        results = (main,) + tuple(small)
        normal, right_side, diagonal = pl.pallas_call(
            hand_on_kernel,
            out_shape=tuple(jax.ShapeDtypeStruct(r.shape, r.dtype) for r in results),
            in_specs=[pl.BlockSpec(memory_space=pl.ANY)] * 3,
            out_specs=(pl.BlockSpec(memory_space=pl.ANY),) * 3,
            scratch_shapes=[pltpu.SemaphoreType.DMA((3,))],
            compiler_params=pltpu.CompilerParams(vmem_limit_bytes=64 * 1024 * 1024),
            name="hand_on",
        )(*results)
        return (normal, right_side.reshape(width), diagonal.reshape(width))
    small = small[0]
    gram = main[:, :width].transpose(1, 0, 2).reshape(width, width)
    owned = lax.psum_scatter(gram, "row", scatter_dimension=0, tiled=True)
    normal = lax.psum_scatter(owned, "grp", scatter_dimension=1, tiled=True)
    small = lax.psum(small, ("grp", "row"))
    row_at = lax.axis_index("row") * normal.shape[0] + lax.broadcasted_iota(
        jnp.int32, normal.shape, 0
    )
    col_at = lax.axis_index("grp") * normal.shape[1] + lax.broadcasted_iota(
        jnp.int32, normal.shape, 1
    )
    normal = jnp.where(row_at == col_at, 0.0, normal * gram_scale)
    right_side = small[:tiles].reshape(width) * gram_scale
    diagonal = small[tiles:].reshape(width) * row_scale
    return (normal, right_side, diagonal)


def solution(mesh):
    placed = (
        P(("grp", "row")),
        P(("grp", "row")),
        P(None, ("grp", "row")),
        P(),
        P(("grp", "row")),
        P(),
    )
    return jax.shard_map(
        on_device,
        mesh=mesh,
        in_specs=placed,
        out_specs=(P("row", "grp"), P(), P()),
        check_vma=False,
    )
```

```python
import functools
import math

import jax
import jax.numpy as jnp
from jax import lax
from jax.experimental import pallas as pl
from jax.experimental.pallas import tpu as pltpu
from jax.sharding import PartitionSpec as P

F32 = jnp.float32
BF16 = jnp.bfloat16
LANES = 128
EXTRA = 16
CHUNK = 64
SIN_C = (4.442866325378418, -7.307384967803955, 3.594230890274048, -0.7829042077064514)
COS_C = (1.41420316696167, -6.977553367614746, 5.714066982269287, -1.7246402502059937)
TURN_HIGH = 2608.0 / 16384.0
TURN_LOW = 1.0 / (2.0 * math.pi) - TURN_HIGH
TURN_UNIT = 2.0**-32
FUSED = True


def poly(u, coefficients):
    total = coefficients[-1]
    for c in coefficients[-2::-1]:
        total = total * u + c
    return total


def nearest(x):
    return (x + 12582912.0) - 12582912.0


def spread(columns, k):
    return jnp.broadcast_to(columns[:, k:k + 1], (LANES, LANES))


def turns(angle):
    head = nearest(angle * 1024.0) * (1.0 / 1024.0)
    tail = angle - head
    coarse = head * TURN_HIGH
    high = nearest(coarse * 32768.0)
    low = (coarse - high * (1.0 / 32768.0)) + (head * TURN_LOW + tail * (TURN_HIGH + TURN_LOW))
    fine = nearest(low * 2.0**32)
    return high.astype(jnp.int32) * 131072 + fine.astype(jnp.int32)


def hand_on_kernel(*refs):
    count = (len(refs) - 1) // 2
    copies = [
        pltpu.make_async_copy(refs[k], refs[count + k], refs[-1].at[k]) for k in range(count)
    ]
    for c in copies:
        c.start()
    for c in copies:
        c.wait()


def local_kernel(
    fused, n_grp, n_row, blocks, taps_n, width, gram_scale, row_scale,
    col_in, lon_in, obs_in, taps_in, seg_in, har_in, *refs,
):
    if fused:
        (out_ref, right_ref, diag_ref, col_ref, lon_ref, obs_got, taps_ref, seg_ref, har_ref, in_sem,
         obs_ref, fresh, window, filt, table, matrix, lab_col, lab, waves, turned, gram,
         halo_send, halo, sa, ra, sb, rb, rs, rr, rx, rz, send_sem, recv_sem) = refs
    else:
        (halo, gram, small_ref, col_ref, lon_ref, obs_got, taps_ref, seg_ref, har_ref, in_sem,
         obs_ref, fresh, window, filt, table, matrix, lab_col, lab, waves, turned) = refs
    per = taps_n // LANES
    own = blocks * per
    col_tiles = width // LANES
    row_index = lax.axis_index("row")
    grp_index = lax.axis_index("grp")

    fetched = (
        (har_in, har_ref), (taps_in, taps_ref), (col_in, col_ref.at[0:own]),
        (lon_in, lon_ref.at[0:own]), (seg_in, seg_ref), (obs_in, obs_got),
    )
    fetches = [
        pltpu.make_async_copy(src, dst, in_sem.at[k]) for k, (src, dst) in enumerate(fetched)
    ]
    for fetch in fetches:
        fetch.start()

    if fused:
        core = lax.rem(row_index, 2)
        z = row_index // 2
        n_z = n_row // 2
        twin = (grp_index, row_index + 1 - 2 * core)
        grp_peers = [(lax.rem(grp_index + k, n_grp), row_index) for k in range(1, n_grp)]
        z_peers = [(grp_index, lax.rem(row_index + 2 * k, n_row)) for k in range(1, n_z)]
        after = (grp_index, lax.rem(row_index + 1, n_row))
        before = (grp_index, lax.rem(row_index + n_row - 1, n_row))
        greeted = [twin, after, before] + [
            (lax.rem(grp_index + dg, n_grp), lax.rem(row_index + 2 * dz, n_row))
            for dg in range(n_grp) for dz in range(n_z) if dg or dz
        ]
        barrier = pltpu.get_barrier_semaphore()
        for peer in greeted:
            pl.semaphore_signal(barrier, inc=1, device_id=peer, device_id_type=pl.DeviceIdType.MESH)

        def copy(src, dst, number, peer):
            c = pltpu.make_async_remote_copy(
                src_ref=src, dst_ref=dst,
                send_sem=send_sem.at[number], recv_sem=recv_sem.at[number],
                device_id=peer, device_id_type=pl.DeviceIdType.MESH,
            )
            c.start()
            return c

    for fetch in fetches:
        fetch.wait()
    obs_ref[:, 0:own * LANES] = obs_got[...].astype(F32)

    if fused:
        last = own - per
        halo_send[0:per] = col_ref[last:last + per]
        halo_send[per:2 * per] = lon_ref[last:last + per]
        halo_send[2 * per:3 * per] = seg_ref[last:last + per].astype(F32)
        for c in range(2):
            for p in range(per):
                at = (last + p) * LANES
                halo_send[(3 + c) * per + p:(3 + c) * per + p + 1] = obs_ref[
                    c:c + 1, at:at + LANES]
        halo_send[5 * per:] = jnp.zeros((halo_send.shape[0] - 5 * per, LANES), F32)

    degree = har_ref[0:1, :].astype(F32)
    order = har_ref[1:2, :]
    size = jnp.abs(order).astype(F32)
    phase = jnp.where(order >= 0, 0.0, -1.0).astype(F32)
    turned[...] = jnp.zeros((LANES, LANES), F32)
    number = 0
    for values in (degree, size, phase):
        for t in range(col_tiles):
            turned[number:number + 1, :] = values[:, t * LANES:(t + 1) * LANES]
            number += 1
    columns = turned[...].T
    for number in range(3):
        for t in range(col_tiles):
            unit = 1 << 30 if number == 2 else 1
            waves[number, t * LANES:(t + 1) * LANES, :] = (
                spread(columns, number * col_tiles + t).astype(jnp.int32) * unit
            )

    below = lax.broadcasted_iota(jnp.int32, (EXTRA, LANES), 0) == 0

    def design_block(slot):
        for half in range(per):
            tile = slot * per + half
            lanes = slice(half * LANES, (half + 1) * LANES)
            theta = turns(col_ref[pl.ds(tile, 1), :])
            phi = turns(lon_ref[pl.ds(tile, 1), :])
            for chunk in range(width // CHUNK):
                rows = slice(chunk * CHUNK, (chunk + 1) * CHUNK)
                a = (waves[0, rows, :] * theta).astype(F32) * TURN_UNIT
                b = (waves[1, rows, :] * phi + waves[2, rows, :]).astype(F32) * TURN_UNIT
                ua = a * a
                ub = b * b
                sin_a = a * poly(ua, SIN_C)
                cos_a = poly(ua, COS_C)
                sin_b = b * poly(ub, SIN_C)
                w = 1.0 - sin_b * sin_b
                sin_w = sin_a * w
                fresh[0, rows, lanes] = (w - sin_a * sin_w).astype(BF16)
                fresh[1, rows, lanes] = (cos_a * sin_w).astype(BF16)
            at = pl.multiple_of(tile * LANES, LANES)
            for c in range(2):
                values = obs_ref[c:c + 1, pl.ds(at, LANES)]
                fresh[c, width:, lanes] = jnp.where(
                    below, jnp.broadcast_to(values, (EXTRA, LANES)), 0.0
                ).astype(BF16)

    def shift():
        window[:, :, taps_n:] = window[:, :, :taps_n]
        window[:, :, :taps_n] = fresh[...]

    window[:, :, :taps_n] = jnp.zeros((2, width + EXTRA, taps_n), BF16)

    @pl.loop(0, 2)
    def _(step):
        design_block(blocks - 1 - step)
        shift()

    if fused:
        pl.semaphore_wait(barrier, len(greeted))
        halo_copy = copy(halo_send, halo, 0, after)

    j = lax.broadcasted_iota(jnp.int32, (taps_n, taps_n), 0)
    i = lax.broadcasted_iota(jnp.int32, (taps_n, taps_n), 1)
    for c in range(2):
        row = jnp.broadcast_to(taps_ref[c:c + 1, :].astype(F32), (8, taps_n))
        base = pltpu.roll(row, 0, 1, stride=1, stride_axis=0)
        for r in range(0, taps_n, 8):
            around = pltpu.roll(base, r, 1) if r else base
            early = i[r:r + 8] < j[r:r + 8]
            table[c, r:r + 8, :] = jnp.where(early, around, 0.0)
            table[c, taps_n + r:taps_n + r + 8, :] = jnp.where(early, 0.0, around)

    first_lane = lax.broadcasted_iota(jnp.int32, (LANES, LANES), 0)
    second_lane = lax.broadcasted_iota(jnp.int32, (LANES, LANES), 1)
    ones = jnp.ones((LANES, LANES), BF16)

    def counted(flags, lanes, rows):
        here = jnp.dot(flags, lanes.astype(BF16), preferred_element_type=F32)
        others = jnp.dot(rows.astype(BF16), flags, preferred_element_type=F32)
        return here + jnp.dot(others.astype(BF16), ones, preferred_element_type=F32)

    first_row = lax.broadcasted_iota(jnp.int32, (own, own), 0)
    second_row = lax.broadcasted_iota(jnp.int32, (own, own), 1)
    lab[0:own] = counted(
        seg_ref[...].astype(F32).astype(BF16), first_lane <= second_lane, second_row < first_row
    )
    if fused:
        halo_copy.wait()
    first_row = lax.broadcasted_iota(jnp.int32, (halo.shape[0], halo.shape[0]), 0)
    second_row = lax.broadcasted_iota(jnp.int32, (halo.shape[0], halo.shape[0]), 1)
    later = (first_row < second_row) & (second_row < 3 * per)
    ahead = counted(halo[...].astype(BF16), first_lane > second_lane, later)
    first = row_index == 0
    lab[own:own + per] = jnp.where(first, -1.0, -ahead[2 * per:3 * per])
    for r in range(per):
        for c in range(2):
            at = (3 + c) * per + r
            obs_ref[c:c + 1, (own + r) * LANES:(own + r + 1) * LANES] = halo[at:at + 1]
    col_ref[own:own + per] = halo[0:per]
    lon_ref[own:own + per] = halo[per:2 * per]
    turned[0:own + per] = lab[...]
    columns = turned[...].T
    for tile in range(own + per):
        lab_col[tile * LANES:(tile + 1) * LANES, :] = spread(columns, tile)

    half_width = width // 2
    half_tiles = half_width // LANES
    gram[...] = jnp.zeros(gram.shape, F32)

    def filter_block(block):
        slots = (lax.rem(block + blocks, blocks + 1), block)
        for half in range(per):
            lanes = slice(half * LANES, (half + 1) * LANES)
            out_label = lab[pl.ds(block * per + half, 1), :]
            for part in range(2 * per):
                at = slice(part * LANES, (part + 1) * LANES)
                tile = slots[part // per] * per + part % per
                got = lab_col[pl.ds(pl.multiple_of(tile * LANES, LANES), LANES), :]
                same = got == out_label
                for c in range(2):
                    matrix[c, at, lanes] = jnp.where(same, table[c, at, lanes], 0.0).astype(BF16)
        for c in range(2):
            filt[:, c * taps_n:(c + 1) * taps_n] = jnp.dot(
                window[c], matrix[c], preferred_element_type=F32
            ).astype(BF16)

    def gram_half(half):
        from_row = half * half_width
        part = lax.dot_general(
            filt[from_row:, :], filt[from_row:from_row + half_width, :],
            (((1,), (1,)), ((), ())), preferred_element_type=F32,
        )
        for t in range(half_tiles):
            gram[half * half_tiles + t, from_row:, :] += part[:, t * LANES:(t + 1) * LANES]

    @pl.loop(0, blocks - 1)
    def _(step):
        block = blocks - 1 - step
        design_block(lax.rem(block - 2 + blocks + 1, blocks + 1))
        filter_block(block)
        gram_half(0)
        gram_half(1)
        shift()

    filter_block(0)
    copies_a = []
    for half in range(2):
        gram_half(half)
        if half == 1:
            for t in range(half_tiles):
                for q in range(half_tiles):
                    gram[half_tiles + t, q * LANES:(q + 1) * LANES, :] = gram[
                        q, half_width + t * LANES:half_width + (t + 1) * LANES, :].T
        if fused:
            tile_rows = width // n_row
            for t in range(half * half_tiles, (half + 1) * half_tiles):
                for zz in range(n_z):
                    at = pl.multiple_of((2 * zz + 1 - core) * tile_rows, tile_rows)
                    sa[t, zz] = gram[t, pl.ds(at, tile_rows), :].astype(BF16)
            part = pl.ds(half * half_tiles, half_tiles)
            copies_a.append(copy(sa.at[part], ra.at[part], 1 + half, twin))

    eye = lax.broadcasted_iota(jnp.int32, (LANES, LANES), 0) == lax.broadcasted_iota(
        jnp.int32, (LANES, LANES), 1
    )
    small = []
    for t in range(col_tiles):
        small.append(gram[t, width:width + 1, :])
    for t in range(col_tiles):
        square = gram[t, t * LANES:(t + 1) * LANES, :]
        small.append(jnp.sum(jnp.where(eye, square, 0.0), axis=0, keepdims=True))
    if not fused:
        for r, row in enumerate(small):
            small_ref[r:r + 1, :] = row
        return

    for r, row in enumerate(small):
        rs[0, r:r + 1, :] = row
    small_a = copy(rs.at[0], rr.at[0], 3, twin)
    for c in copies_a:
        c.wait()
    for t in range(col_tiles):
        for zz in range(n_z):
            at = pl.multiple_of((2 * zz + core) * tile_rows, tile_rows)
            gram[t, pl.ds(zz * tile_rows, tile_rows), :] = gram[
                t, pl.ds(at, tile_rows), :] + ra[t, zz].astype(F32)

    def held(t, zz):
        return gram[t, pl.ds(pl.multiple_of(zz * tile_rows, tile_rows), tile_rows), :]

    small_a.wait()
    rx[grp_index] = rs[0] + rr[0]
    small_b = [
        copy(rx.at[grp_index], rx.at[grp_index], 3 + k, grp_peers[k - 1]) for k in range(1, n_grp)
    ]
    offsets = [(dg, dz) for dz in (2, 1, 3, 0) for dg in (3, 2, 1, 0) if dg or dz]
    copies_b = []
    for dg, dz in offsets:
        slot = dg * n_z + dz
        there = (lax.rem(grp_index + dg, n_grp), lax.rem(z + dz, n_z))
        sb[slot] = held(*there).astype(BF16)
        copies_b.append(copy(
            sb.at[slot], rb.at[slot], 10 + slot, (there[0], 2 * there[1] + core)
        ))
    for c in small_b:
        c.wait()
    total = rx[0]
    for g in range(1, n_grp):
        total = total + rx[g]
    rz[z] = total
    small_d = [copy(rz.at[z], rz.at[z], 6 + k, z_peers[k - 1]) for k in range(1, n_z)]
    total = held(grp_index, z)
    for (dg, dz), c in zip(offsets, copies_b):
        c.wait()
        total = total + rb[dg * n_z + dz].astype(F32)
    row_at = row_index * tile_rows + lax.broadcasted_iota(jnp.int32, total.shape, 0)
    col_at = grp_index * LANES + lax.broadcasted_iota(jnp.int32, total.shape, 1)
    out_ref[...] = jnp.where(row_at == col_at, 0.0, total * gram_scale)
    for c in small_d:
        c.wait()
    total = rz[0]
    for zz in range(1, n_z):
        total = total + rz[zz]
    right_ref[...] = total[0:col_tiles] * gram_scale
    diag_ref[...] = total[col_tiles:] * row_scale


def on_device(colatitude, longitude, observed, filter_taps, segment_start, harmonic):
    rows_here = colatitude.shape[0]
    taps_n = filter_taps.shape[1]
    width = harmonic.shape[1]
    n_grp = lax.axis_size("grp")
    n_row = lax.axis_size("row")
    blocks = rows_here // taps_n
    per = taps_n // LANES
    tiles = width // LANES
    rows_total = rows_here * n_grp * n_row
    row_scale = 1.0 / rows_total
    gram_scale = 1.0 / math.sqrt(rows_total)
    fused = FUSED and n_grp == 4 and n_row == 8 and width == n_grp * LANES
    split = [a.reshape(rows_here // LANES, LANES) for a in (colatitude, longitude, segment_start)]
    inputs = [split[0], split[1], observed, filter_taps, split[2], harmonic]
    window = rows_here + taps_n
    scratch = [
        pltpu.VMEM((window // LANES, LANES), F32),
        pltpu.VMEM((window // LANES, LANES), F32),
        pltpu.VMEM(observed.shape, observed.dtype),
        pltpu.VMEM(filter_taps.shape, filter_taps.dtype),
        pltpu.VMEM((rows_here // LANES, LANES), segment_start.dtype),
        pltpu.VMEM(harmonic.shape, harmonic.dtype),
        pltpu.SemaphoreType.DMA((6,)),
        pltpu.VMEM((2, window), F32),
        pltpu.VMEM((2, width + EXTRA, taps_n), BF16),
        pltpu.VMEM((2, width + EXTRA, 2 * taps_n), BF16),
        pltpu.VMEM((width + EXTRA, 2 * taps_n), BF16),
        pltpu.VMEM((2, 2 * taps_n, taps_n), F32),
        pltpu.VMEM((2, 2 * taps_n, taps_n), BF16),
        pltpu.VMEM((window, LANES), F32),
        pltpu.VMEM((window // LANES, LANES), F32),
        pltpu.VMEM((3, width, LANES), jnp.int32),
        pltpu.VMEM((LANES, LANES), F32),
    ]
    gram_shape = (tiles, width + EXTRA, LANES)
    small_shapes = (jax.ShapeDtypeStruct((2 * tiles, LANES), F32),)
    halo_shape = (8 * per, LANES)
    if fused:
        tile_rows = width // n_row
        n_z = n_row // 2
        tile = (tile_rows, LANES)
        copies = 10 + n_grp * n_z
        scratch += [
            pltpu.VMEM(gram_shape, F32),
            pltpu.VMEM(halo_shape, F32),
            pltpu.VMEM(halo_shape, F32),
            pltpu.VMEM((tiles, n_z) + tile, BF16),
            pltpu.VMEM((tiles, n_z) + tile, BF16),
            pltpu.VMEM((n_grp * n_z,) + tile, BF16),
            pltpu.VMEM((n_grp * n_z,) + tile, BF16),
            pltpu.VMEM((1, 2 * tiles, LANES), F32),
            pltpu.VMEM((1, 2 * tiles, LANES), F32),
            pltpu.VMEM((n_grp, 2 * tiles, LANES), F32),
            pltpu.VMEM((n_z, 2 * tiles, LANES), F32),
            pltpu.SemaphoreType.DMA((copies,)),
            pltpu.SemaphoreType.DMA((copies,)),
        ]
        main_shape = jax.ShapeDtypeStruct((tile_rows, LANES), F32)
        small_shapes = (jax.ShapeDtypeStruct((tiles, LANES), F32),) * 2
    else:
        last = rows_here // LANES - per
        pieces = [split[0][last:], split[1][last:], split[2][last:].astype(F32)]
        pieces.append(observed[:, rows_here - taps_n:].astype(F32).reshape(2 * per, LANES))
        pieces.append(jnp.zeros((3 * per, LANES), F32))
        pairs = [(k, k + 1) for k in range(n_row - 1)]
        inputs.append(lax.ppermute(jnp.concatenate(pieces), "row", pairs))
        main_shape = jax.ShapeDtypeStruct(gram_shape, F32)
    params = dict(vmem_limit_bytes=64 * 1024 * 1024)
    if fused:
        params.update(collective_id=0, has_side_effects=True)
    main, *small = pl.pallas_call(
        functools.partial(
            local_kernel, fused, n_grp, n_row, blocks, taps_n, width, gram_scale, row_scale
        ),
        out_shape=(main_shape,) + small_shapes,
        in_specs=[pl.BlockSpec(memory_space=pltpu.HBM)] * 6
        + [pl.BlockSpec(memory_space=pltpu.VMEM)] * (len(inputs) - 6),
        out_specs=(pl.BlockSpec(memory_space=pltpu.VMEM),) * (1 + len(small_shapes)),
        scratch_shapes=scratch,
        compiler_params=pltpu.CompilerParams(**params),
        name="normal_equations",
    )(*inputs)
    if fused:
        results = (main,) + tuple(small)
        normal, right_side, diagonal = pl.pallas_call(
            hand_on_kernel,
            out_shape=tuple(jax.ShapeDtypeStruct(r.shape, r.dtype) for r in results),
            in_specs=[pl.BlockSpec(memory_space=pl.ANY)] * 3,
            out_specs=(pl.BlockSpec(memory_space=pl.ANY),) * 3,
            scratch_shapes=[pltpu.SemaphoreType.DMA((3,))],
            compiler_params=pltpu.CompilerParams(vmem_limit_bytes=64 * 1024 * 1024),
            name="hand_on",
        )(*results)
        return (normal, right_side.reshape(width), diagonal.reshape(width))
    small = small[0]
    gram = main[:, :width].transpose(1, 0, 2).reshape(width, width)
    owned = lax.psum_scatter(gram, "row", scatter_dimension=0, tiled=True)
    normal = lax.psum_scatter(owned, "grp", scatter_dimension=1, tiled=True)
    small = lax.psum(small, ("grp", "row"))
    row_at = lax.axis_index("row") * normal.shape[0] + lax.broadcasted_iota(
        jnp.int32, normal.shape, 0
    )
    col_at = lax.axis_index("grp") * normal.shape[1] + lax.broadcasted_iota(
        jnp.int32, normal.shape, 1
    )
    normal = jnp.where(row_at == col_at, 0.0, normal * gram_scale)
    right_side = small[:tiles].reshape(width) * gram_scale
    diagonal = small[tiles:].reshape(width) * row_scale
    return (normal, right_side, diagonal)


def solution(mesh):
    placed = (
        P(("grp", "row")),
        P(("grp", "row")),
        P(None, ("grp", "row")),
        P(),
        P(("grp", "row")),
        P(),
    )
    return jax.shard_map(
        on_device,
        mesh=mesh,
        in_specs=placed,
        out_specs=(P("row", "grp"), P(), P()),
        check_vma=False,
    )
```

```python
import functools
import math

import jax
import jax.numpy as jnp
from jax import lax
from jax.experimental import pallas as pl
from jax.experimental.pallas import tpu as pltpu
from jax.sharding import PartitionSpec as P

F32 = jnp.float32
BF16 = jnp.bfloat16
LANES = 128
EXTRA = 16
CHUNK = 64
SIN_C = (4.442866325378418, -7.307384967803955, 3.594230890274048, -0.7829042077064514)
COS_C = (1.41420316696167, -6.977553367614746, 5.714066982269287, -1.7246402502059937)
TURN_HIGH = 2608.0 / 16384.0
TURN_LOW = 1.0 / (2.0 * math.pi) - TURN_HIGH
FUSED = True


def poly(u, coefficients):
    total = coefficients[-1]
    for c in coefficients[-2::-1]:
        total = total * u + c
    return total


def nearest(x):
    return (x + 12582912.0) - 12582912.0


def spread(columns, k):
    return jnp.broadcast_to(columns[:, k:k + 1], (LANES, LANES))


def turns(angle):
    head = nearest(angle * 1024.0) * (1.0 / 1024.0)
    tail = angle - head
    return head * TURN_HIGH + (head * TURN_LOW + tail * (TURN_HIGH + TURN_LOW))


def hand_on_kernel(*refs):
    count = (len(refs) - 1) // 2
    copies = [
        pltpu.make_async_copy(refs[k], refs[count + k], refs[-1].at[k]) for k in range(count)
    ]
    for c in copies:
        c.start()
    for c in copies:
        c.wait()


def local_kernel(
    fused, n_grp, n_row, blocks, taps_n, width, gram_scale, row_scale,
    col_in, lon_in, obs_in, taps_in, seg_in, har_in, *refs,
):
    if fused:
        (out_ref, right_ref, diag_ref, col_ref, lon_ref, obs_got, taps_ref, seg_ref, har_ref, in_sem,
         obs_ref, fresh, window, filt, table, matrix, lab_col, lab, waves, turned, gram,
         halo_send, halo, sa, ra, sb, rb, rs, rr, rx, rz, send_sem, recv_sem) = refs
    else:
        (halo, gram, small_ref, col_ref, lon_ref, obs_got, taps_ref, seg_ref, har_ref, in_sem,
         obs_ref, fresh, window, filt, table, matrix, lab_col, lab, waves, turned) = refs
    per = taps_n // LANES
    own = blocks * per
    col_tiles = width // LANES
    row_index = lax.axis_index("row")
    grp_index = lax.axis_index("grp")

    fetched = (
        (har_in, har_ref), (taps_in, taps_ref), (col_in, col_ref.at[0:own]),
        (lon_in, lon_ref.at[0:own]), (seg_in, seg_ref), (obs_in, obs_got),
    )
    fetches = [
        pltpu.make_async_copy(src, dst, in_sem.at[k]) for k, (src, dst) in enumerate(fetched)
    ]
    for fetch in fetches:
        fetch.start()

    if fused:
        core = lax.rem(row_index, 2)
        z = row_index // 2
        n_z = n_row // 2
        twin = (grp_index, row_index + 1 - 2 * core)
        grp_peers = [(lax.rem(grp_index + k, n_grp), row_index) for k in range(1, n_grp)]
        z_peers = [(grp_index, lax.rem(row_index + 2 * k, n_row)) for k in range(1, n_z)]
        after = (grp_index, lax.rem(row_index + 1, n_row))
        before = (grp_index, lax.rem(row_index + n_row - 1, n_row))
        greeted = [twin, after, before] + [
            (lax.rem(grp_index + dg, n_grp), lax.rem(row_index + 2 * dz, n_row))
            for dg in range(n_grp) for dz in range(n_z) if dg or dz
        ]
        barrier = pltpu.get_barrier_semaphore()
        for peer in greeted:
            pl.semaphore_signal(barrier, inc=1, device_id=peer, device_id_type=pl.DeviceIdType.MESH)

        def copy(src, dst, number, peer):
            c = pltpu.make_async_remote_copy(
                src_ref=src, dst_ref=dst,
                send_sem=send_sem.at[number], recv_sem=recv_sem.at[number],
                device_id=peer, device_id_type=pl.DeviceIdType.MESH,
            )
            c.start()
            return c

    for fetch in fetches:
        fetch.wait()
    obs_ref[:, 0:own * LANES] = obs_got[...].astype(F32)

    if fused:
        last = own - per
        halo_send[0:per] = col_ref[last:last + per]
        halo_send[per:2 * per] = lon_ref[last:last + per]
        halo_send[2 * per:3 * per] = seg_ref[last:last + per].astype(F32)
        for c in range(2):
            for p in range(per):
                at = (last + p) * LANES
                halo_send[(3 + c) * per + p:(3 + c) * per + p + 1] = obs_ref[
                    c:c + 1, at:at + LANES]
        halo_send[5 * per:] = jnp.zeros((halo_send.shape[0] - 5 * per, LANES), F32)

    degree = har_ref[0:1, :].astype(F32)
    order = har_ref[1:2, :]
    size = jnp.abs(order).astype(F32)
    phase = jnp.where(order >= 0, 0.0, -0.25).astype(F32)
    turned[...] = jnp.zeros((LANES, LANES), F32)
    number = 0
    for values in (degree, size, phase):
        for t in range(col_tiles):
            turned[number:number + 1, :] = values[:, t * LANES:(t + 1) * LANES]
            number += 1
    columns = turned[...].T
    for number in range(3):
        for t in range(col_tiles):
            waves[number, t * LANES:(t + 1) * LANES, :] = spread(columns, number * col_tiles + t)

    below = lax.broadcasted_iota(jnp.int32, (EXTRA, LANES), 0) == 0

    def design_block(slot):
        for half in range(per):
            tile = slot * per + half
            lanes = slice(half * LANES, (half + 1) * LANES)
            theta = turns(col_ref[pl.ds(tile, 1), :])
            phi = turns(lon_ref[pl.ds(tile, 1), :])
            for chunk in range(width // CHUNK):
                rows = slice(chunk * CHUNK, (chunk + 1) * CHUNK)
                a = waves[0, rows, :] * theta
                b = waves[1, rows, :] * phi + waves[2, rows, :]
                a = a - nearest(a)
                b = b - nearest(b)
                ua = a * a
                ub = b * b
                sin_a = a * poly(ua, SIN_C)
                cos_a = poly(ua, COS_C)
                sin_b = b * poly(ub, SIN_C)
                w = 1.0 - sin_b * sin_b
                sin_w = sin_a * w
                fresh[0, rows, lanes] = (w - sin_a * sin_w).astype(BF16)
                fresh[1, rows, lanes] = (cos_a * sin_w).astype(BF16)
            at = pl.multiple_of(tile * LANES, LANES)
            for c in range(2):
                values = obs_ref[c:c + 1, pl.ds(at, LANES)]
                fresh[c, width:, lanes] = jnp.where(
                    below, jnp.broadcast_to(values, (EXTRA, LANES)), 0.0
                ).astype(BF16)

    def shift():
        window[:, :, taps_n:] = window[:, :, :taps_n]
        window[:, :, :taps_n] = fresh[...]

    window[:, :, :taps_n] = jnp.zeros((2, width + EXTRA, taps_n), BF16)

    @pl.loop(0, 2)
    def _(step):
        design_block(blocks - 1 - step)
        shift()

    if fused:
        pl.semaphore_wait(barrier, len(greeted))
        halo_copy = copy(halo_send, halo, 0, after)

    j = lax.broadcasted_iota(jnp.int32, (taps_n, taps_n), 0)
    i = lax.broadcasted_iota(jnp.int32, (taps_n, taps_n), 1)
    for c in range(2):
        row = jnp.broadcast_to(taps_ref[c:c + 1, :].astype(F32), (8, taps_n))
        base = pltpu.roll(row, 0, 1, stride=1, stride_axis=0)
        for r in range(0, taps_n, 8):
            around = pltpu.roll(base, r, 1) if r else base
            early = i[r:r + 8] < j[r:r + 8]
            table[c, r:r + 8, :] = jnp.where(early, around, 0.0)
            table[c, taps_n + r:taps_n + r + 8, :] = jnp.where(early, 0.0, around)

    first_lane = lax.broadcasted_iota(jnp.int32, (LANES, LANES), 0)
    second_lane = lax.broadcasted_iota(jnp.int32, (LANES, LANES), 1)
    ones = jnp.ones((LANES, LANES), BF16)

    def counted(flags, lanes, rows):
        here = jnp.dot(flags, lanes.astype(BF16), preferred_element_type=F32)
        others = jnp.dot(rows.astype(BF16), flags, preferred_element_type=F32)
        return here + jnp.dot(others.astype(BF16), ones, preferred_element_type=F32)

    first_row = lax.broadcasted_iota(jnp.int32, (own, own), 0)
    second_row = lax.broadcasted_iota(jnp.int32, (own, own), 1)
    lab[0:own] = counted(
        seg_ref[...].astype(F32).astype(BF16), first_lane <= second_lane, second_row < first_row
    )
    if fused:
        halo_copy.wait()
    first_row = lax.broadcasted_iota(jnp.int32, (halo.shape[0], halo.shape[0]), 0)
    second_row = lax.broadcasted_iota(jnp.int32, (halo.shape[0], halo.shape[0]), 1)
    later = (first_row < second_row) & (second_row < 3 * per)
    ahead = counted(halo[...].astype(BF16), first_lane > second_lane, later)
    first = row_index == 0
    lab[own:own + per] = jnp.where(first, -1.0, -ahead[2 * per:3 * per])
    for r in range(per):
        for c in range(2):
            at = (3 + c) * per + r
            obs_ref[c:c + 1, (own + r) * LANES:(own + r + 1) * LANES] = halo[at:at + 1]
    col_ref[own:own + per] = halo[0:per]
    lon_ref[own:own + per] = halo[per:2 * per]
    turned[0:own + per] = lab[...]
    columns = turned[...].T
    for tile in range(own + per):
        lab_col[tile * LANES:(tile + 1) * LANES, :] = spread(columns, tile)

    half_width = width // 2
    half_tiles = half_width // LANES
    gram[...] = jnp.zeros(gram.shape, F32)

    def filter_block(block):
        slots = (lax.rem(block + blocks, blocks + 1), block)
        for half in range(per):
            lanes = slice(half * LANES, (half + 1) * LANES)
            out_label = lab[pl.ds(block * per + half, 1), :]
            for part in range(2 * per):
                at = slice(part * LANES, (part + 1) * LANES)
                tile = slots[part // per] * per + part % per
                got = lab_col[pl.ds(pl.multiple_of(tile * LANES, LANES), LANES), :]
                same = got == out_label
                for c in range(2):
                    matrix[c, at, lanes] = jnp.where(same, table[c, at, lanes], 0.0).astype(BF16)
        for c in range(2):
            filt[:, c * taps_n:(c + 1) * taps_n] = jnp.dot(
                window[c], matrix[c], preferred_element_type=F32
            ).astype(BF16)

    def gram_half(half):
        from_row = half * half_width
        part = lax.dot_general(
            filt[from_row:, :], filt[from_row:from_row + half_width, :],
            (((1,), (1,)), ((), ())), preferred_element_type=F32,
        )
        for t in range(half_tiles):
            gram[half * half_tiles + t, from_row:, :] += part[:, t * LANES:(t + 1) * LANES]

    @pl.loop(0, blocks - 1)
    def _(step):
        block = blocks - 1 - step
        design_block(lax.rem(block - 2 + blocks + 1, blocks + 1))
        filter_block(block)
        gram_half(0)
        gram_half(1)
        shift()

    filter_block(0)
    copies_a = []
    for half in range(2):
        gram_half(half)
        if half == 1:
            for t in range(half_tiles):
                for q in range(half_tiles):
                    gram[half_tiles + t, q * LANES:(q + 1) * LANES, :] = gram[
                        q, half_width + t * LANES:half_width + (t + 1) * LANES, :].T
        if fused:
            tile_rows = width // n_row
            for t in range(half * half_tiles, (half + 1) * half_tiles):
                for zz in range(n_z):
                    at = pl.multiple_of((2 * zz + 1 - core) * tile_rows, tile_rows)
                    sa[t, zz] = gram[t, pl.ds(at, tile_rows), :].astype(BF16)
            part = pl.ds(half * half_tiles, half_tiles)
            copies_a.append(copy(sa.at[part], ra.at[part], 1 + half, twin))

    eye = lax.broadcasted_iota(jnp.int32, (LANES, LANES), 0) == lax.broadcasted_iota(
        jnp.int32, (LANES, LANES), 1
    )
    small = []
    for t in range(col_tiles):
        small.append(gram[t, width:width + 1, :])
    for t in range(col_tiles):
        square = gram[t, t * LANES:(t + 1) * LANES, :]
        small.append(jnp.sum(jnp.where(eye, square, 0.0), axis=0, keepdims=True))
    if not fused:
        for r, row in enumerate(small):
            small_ref[r:r + 1, :] = row
        return

    for r, row in enumerate(small):
        rs[0, r:r + 1, :] = row
    small_a = copy(rs.at[0], rr.at[0], 3, twin)
    for c in copies_a:
        c.wait()
    for t in range(col_tiles):
        for zz in range(n_z):
            at = pl.multiple_of((2 * zz + core) * tile_rows, tile_rows)
            gram[t, pl.ds(zz * tile_rows, tile_rows), :] = gram[
                t, pl.ds(at, tile_rows), :] + ra[t, zz].astype(F32)

    def held(t, zz):
        return gram[t, pl.ds(pl.multiple_of(zz * tile_rows, tile_rows), tile_rows), :]

    small_a.wait()
    rx[grp_index] = rs[0] + rr[0]
    small_b = [
        copy(rx.at[grp_index], rx.at[grp_index], 3 + k, grp_peers[k - 1]) for k in range(1, n_grp)
    ]
    offsets = [(dg, dz) for dz in (2, 1, 3, 0) for dg in (3, 2, 1, 0) if dg or dz]
    copies_b = []
    for dg, dz in offsets:
        slot = dg * n_z + dz
        there = (lax.rem(grp_index + dg, n_grp), lax.rem(z + dz, n_z))
        sb[slot] = held(*there).astype(BF16)
        copies_b.append(copy(
            sb.at[slot], rb.at[slot], 10 + slot, (there[0], 2 * there[1] + core)
        ))
    for c in small_b:
        c.wait()
    total = rx[0]
    for g in range(1, n_grp):
        total = total + rx[g]
    rz[z] = total
    small_d = [copy(rz.at[z], rz.at[z], 6 + k, z_peers[k - 1]) for k in range(1, n_z)]
    total = held(grp_index, z)
    for (dg, dz), c in zip(offsets, copies_b):
        c.wait()
        total = total + rb[dg * n_z + dz].astype(F32)
    row_at = row_index * tile_rows + lax.broadcasted_iota(jnp.int32, total.shape, 0)
    col_at = grp_index * LANES + lax.broadcasted_iota(jnp.int32, total.shape, 1)
    out_ref[...] = jnp.where(row_at == col_at, 0.0, total * gram_scale)
    for c in small_d:
        c.wait()
    total = rz[0]
    for zz in range(1, n_z):
        total = total + rz[zz]
    right_ref[...] = total[0:col_tiles] * gram_scale
    diag_ref[...] = total[col_tiles:] * row_scale


def on_device(colatitude, longitude, observed, filter_taps, segment_start, harmonic):
    rows_here = colatitude.shape[0]
    taps_n = filter_taps.shape[1]
    width = harmonic.shape[1]
    n_grp = lax.axis_size("grp")
    n_row = lax.axis_size("row")
    blocks = rows_here // taps_n
    per = taps_n // LANES
    tiles = width // LANES
    rows_total = rows_here * n_grp * n_row
    row_scale = 1.0 / rows_total
    gram_scale = 1.0 / math.sqrt(rows_total)
    fused = FUSED and n_grp == 4 and n_row == 8 and width == n_grp * LANES
    split = [a.reshape(rows_here // LANES, LANES) for a in (colatitude, longitude, segment_start)]
    inputs = [split[0], split[1], observed, filter_taps, split[2], harmonic]
    window = rows_here + taps_n
    scratch = [
        pltpu.VMEM((window // LANES, LANES), F32),
        pltpu.VMEM((window // LANES, LANES), F32),
        pltpu.VMEM(observed.shape, observed.dtype),
        pltpu.VMEM(filter_taps.shape, filter_taps.dtype),
        pltpu.VMEM((rows_here // LANES, LANES), segment_start.dtype),
        pltpu.VMEM(harmonic.shape, harmonic.dtype),
        pltpu.SemaphoreType.DMA((6,)),
        pltpu.VMEM((2, window), F32),
        pltpu.VMEM((2, width + EXTRA, taps_n), BF16),
        pltpu.VMEM((2, width + EXTRA, 2 * taps_n), BF16),
        pltpu.VMEM((width + EXTRA, 2 * taps_n), BF16),
        pltpu.VMEM((2, 2 * taps_n, taps_n), F32),
        pltpu.VMEM((2, 2 * taps_n, taps_n), BF16),
        pltpu.VMEM((window, LANES), F32),
        pltpu.VMEM((window // LANES, LANES), F32),
        pltpu.VMEM((3, width, LANES), F32),
        pltpu.VMEM((LANES, LANES), F32),
    ]
    gram_shape = (tiles, width + EXTRA, LANES)
    small_shapes = (jax.ShapeDtypeStruct((2 * tiles, LANES), F32),)
    halo_shape = (8 * per, LANES)
    if fused:
        tile_rows = width // n_row
        n_z = n_row // 2
        tile = (tile_rows, LANES)
        copies = 10 + n_grp * n_z
        scratch += [
            pltpu.VMEM(gram_shape, F32),
            pltpu.VMEM(halo_shape, F32),
            pltpu.VMEM(halo_shape, F32),
            pltpu.VMEM((tiles, n_z) + tile, BF16),
            pltpu.VMEM((tiles, n_z) + tile, BF16),
            pltpu.VMEM((n_grp * n_z,) + tile, BF16),
            pltpu.VMEM((n_grp * n_z,) + tile, BF16),
            pltpu.VMEM((1, 2 * tiles, LANES), F32),
            pltpu.VMEM((1, 2 * tiles, LANES), F32),
            pltpu.VMEM((n_grp, 2 * tiles, LANES), F32),
            pltpu.VMEM((n_z, 2 * tiles, LANES), F32),
            pltpu.SemaphoreType.DMA((copies,)),
            pltpu.SemaphoreType.DMA((copies,)),
        ]
        main_shape = jax.ShapeDtypeStruct((tile_rows, LANES), F32)
        small_shapes = (jax.ShapeDtypeStruct((tiles, LANES), F32),) * 2
    else:
        last = rows_here // LANES - per
        pieces = [split[0][last:], split[1][last:], split[2][last:].astype(F32)]
        pieces.append(observed[:, rows_here - taps_n:].astype(F32).reshape(2 * per, LANES))
        pieces.append(jnp.zeros((3 * per, LANES), F32))
        pairs = [(k, k + 1) for k in range(n_row - 1)]
        inputs.append(lax.ppermute(jnp.concatenate(pieces), "row", pairs))
        main_shape = jax.ShapeDtypeStruct(gram_shape, F32)
    params = dict(vmem_limit_bytes=64 * 1024 * 1024)
    if fused:
        params.update(collective_id=0, has_side_effects=True)
    main, *small = pl.pallas_call(
        functools.partial(
            local_kernel, fused, n_grp, n_row, blocks, taps_n, width, gram_scale, row_scale
        ),
        out_shape=(main_shape,) + small_shapes,
        in_specs=[pl.BlockSpec(memory_space=pltpu.HBM)] * 6
        + [pl.BlockSpec(memory_space=pltpu.VMEM)] * (len(inputs) - 6),
        out_specs=(pl.BlockSpec(memory_space=pltpu.VMEM),) * (1 + len(small_shapes)),
        scratch_shapes=scratch,
        compiler_params=pltpu.CompilerParams(**params),
        name="normal_equations",
    )(*inputs)
    if fused:
        results = (main,) + tuple(small)
        normal, right_side, diagonal = pl.pallas_call(
            hand_on_kernel,
            out_shape=tuple(jax.ShapeDtypeStruct(r.shape, r.dtype) for r in results),
            in_specs=[pl.BlockSpec(memory_space=pl.ANY)] * 3,
            out_specs=(pl.BlockSpec(memory_space=pl.ANY),) * 3,
            scratch_shapes=[pltpu.SemaphoreType.DMA((3,))],
            compiler_params=pltpu.CompilerParams(vmem_limit_bytes=64 * 1024 * 1024),
            name="hand_on",
        )(*results)
        return (normal, right_side.reshape(width), diagonal.reshape(width))
    small = small[0]
    gram = main[:, :width].transpose(1, 0, 2).reshape(width, width)
    owned = lax.psum_scatter(gram, "row", scatter_dimension=0, tiled=True)
    normal = lax.psum_scatter(owned, "grp", scatter_dimension=1, tiled=True)
    small = lax.psum(small, ("grp", "row"))
    row_at = lax.axis_index("row") * normal.shape[0] + lax.broadcasted_iota(
        jnp.int32, normal.shape, 0
    )
    col_at = lax.axis_index("grp") * normal.shape[1] + lax.broadcasted_iota(
        jnp.int32, normal.shape, 1
    )
    normal = jnp.where(row_at == col_at, 0.0, normal * gram_scale)
    right_side = small[:tiles].reshape(width) * gram_scale
    diagonal = small[tiles:].reshape(width) * row_scale
    return (normal, right_side, diagonal)


def solution(mesh):
    placed = (
        P(("grp", "row")),
        P(("grp", "row")),
        P(None, ("grp", "row")),
        P(),
        P(("grp", "row")),
        P(),
    )
    return jax.shard_map(
        on_device,
        mesh=mesh,
        in_specs=placed,
        out_specs=(P("row", "grp"), P(), P()),
        check_vma=False,
    )
```

```python
import functools
import math

import jax
import jax.numpy as jnp
from jax import lax
from jax.experimental import pallas as pl
from jax.experimental.pallas import tpu as pltpu
from jax.sharding import PartitionSpec as P

F32 = jnp.float32
BF16 = jnp.bfloat16
LANES = 128
EXTRA = 16
CHUNK = 64
SIN_C = (4.442866325378418, -7.307384967803955, 3.594230890274048, -0.7829042077064514)
COS_C = (1.41420316696167, -6.977553367614746, 5.714066982269287, -1.7246402502059937)
TURN_HIGH = 2608.0 / 16384.0
TURN_LOW = 1.0 / (2.0 * math.pi) - TURN_HIGH
TURN_UNIT = 2.0**-32
FUSED = True


def poly(u, coefficients):
    total = coefficients[-1]
    for c in coefficients[-2::-1]:
        total = total * u + c
    return total


def nearest(x):
    return (x + 12582912.0) - 12582912.0


def spread(columns, k):
    return jnp.broadcast_to(columns[:, k:k + 1], (LANES, LANES))


def turns(angle):
    head = nearest(angle * 1024.0) * (1.0 / 1024.0)
    tail = angle - head
    coarse = head * TURN_HIGH
    high = nearest(coarse * 32768.0)
    low = (coarse - high * (1.0 / 32768.0)) + (head * TURN_LOW + tail * (TURN_HIGH + TURN_LOW))
    fine = nearest(low * 2.0**32)
    return high.astype(jnp.int32) * 131072 + fine.astype(jnp.int32)


def hand_on_kernel(*refs):
    count = (len(refs) - 1) // 2
    copies = [
        pltpu.make_async_copy(refs[k], refs[count + k], refs[-1].at[k]) for k in range(count)
    ]
    for c in copies:
        c.start()
    for c in copies:
        c.wait()


def local_kernel(
    fused, n_grp, n_row, blocks, taps_n, width, gram_scale, row_scale,
    col_in, lon_in, obs_in, taps_in, seg_in, har_in, *refs,
):
    if fused:
        (out_ref, right_ref, diag_ref, col_ref, lon_ref, obs_got, taps_ref, seg_ref, har_ref, in_sem,
         obs_ref, fresh, window, filt, filt_next, table, matrix, lab_col, lab, waves, turned, gram,
         halo_send, halo, sa, ra, sb, rb, rs, rr, rx, rz, send_sem, recv_sem) = refs
    else:
        (halo, gram, small_ref, col_ref, lon_ref, obs_got, taps_ref, seg_ref, har_ref, in_sem,
         obs_ref, fresh, window, filt, filt_next, table, matrix, lab_col, lab, waves, turned) = refs
    per = taps_n // LANES
    own = blocks * per
    col_tiles = width // LANES
    row_index = lax.axis_index("row")
    grp_index = lax.axis_index("grp")

    fetched = (
        (har_in, har_ref), (taps_in, taps_ref), (col_in, col_ref.at[0:own]),
        (lon_in, lon_ref.at[0:own]), (seg_in, seg_ref), (obs_in, obs_got),
    )
    fetches = [
        pltpu.make_async_copy(src, dst, in_sem.at[k]) for k, (src, dst) in enumerate(fetched)
    ]
    for fetch in fetches:
        fetch.start()

    if fused:
        core = lax.rem(row_index, 2)
        z = row_index // 2
        n_z = n_row // 2
        twin = (grp_index, row_index + 1 - 2 * core)
        grp_peers = [(lax.rem(grp_index + k, n_grp), row_index) for k in range(1, n_grp)]
        z_peers = [(grp_index, lax.rem(row_index + 2 * k, n_row)) for k in range(1, n_z)]
        after = (grp_index, lax.rem(row_index + 1, n_row))
        before = (grp_index, lax.rem(row_index + n_row - 1, n_row))
        greeted = [twin, after, before] + [
            (lax.rem(grp_index + dg, n_grp), lax.rem(row_index + 2 * dz, n_row))
            for dg in range(n_grp) for dz in range(n_z) if dg or dz
        ]
        barrier = pltpu.get_barrier_semaphore()
        for peer in greeted:
            pl.semaphore_signal(barrier, inc=1, device_id=peer, device_id_type=pl.DeviceIdType.MESH)

        def copy(src, dst, number, peer):
            c = pltpu.make_async_remote_copy(
                src_ref=src, dst_ref=dst,
                send_sem=send_sem.at[number], recv_sem=recv_sem.at[number],
                device_id=peer, device_id_type=pl.DeviceIdType.MESH,
            )
            c.start()
            return c

    for fetch in fetches:
        fetch.wait()
    obs_ref[:, 0:own * LANES] = obs_got[...].astype(F32)

    if fused:
        last = own - per
        halo_send[0:per] = col_ref[last:last + per]
        halo_send[per:2 * per] = lon_ref[last:last + per]
        halo_send[2 * per:3 * per] = seg_ref[last:last + per].astype(F32)
        for c in range(2):
            for p in range(per):
                at = (last + p) * LANES
                halo_send[(3 + c) * per + p:(3 + c) * per + p + 1] = obs_ref[
                    c:c + 1, at:at + LANES]
        halo_send[5 * per:] = jnp.zeros((halo_send.shape[0] - 5 * per, LANES), F32)

    degree = har_ref[0:1, :].astype(F32)
    order = har_ref[1:2, :]
    size = jnp.abs(order).astype(F32)
    phase = jnp.where(order >= 0, 0.0, -1.0).astype(F32)
    turned[...] = jnp.zeros((LANES, LANES), F32)
    number = 0
    for values in (degree, size, phase):
        for t in range(col_tiles):
            turned[number:number + 1, :] = values[:, t * LANES:(t + 1) * LANES]
            number += 1
    columns = turned[...].T
    for number in range(3):
        for t in range(col_tiles):
            unit = 1 << 30 if number == 2 else 1
            waves[number, t * LANES:(t + 1) * LANES, :] = (
                spread(columns, number * col_tiles + t).astype(jnp.int32) * unit
            )

    below = lax.broadcasted_iota(jnp.int32, (EXTRA, LANES), 0) == 0

    def design_block(slot):
        for half in range(per):
            tile = slot * per + half
            lanes = slice(half * LANES, (half + 1) * LANES)
            theta = turns(col_ref[pl.ds(tile, 1), :])
            phi = turns(lon_ref[pl.ds(tile, 1), :])
            for chunk in range(width // CHUNK):
                rows = slice(chunk * CHUNK, (chunk + 1) * CHUNK)
                a = (waves[0, rows, :] * theta).astype(F32) * TURN_UNIT
                b = (waves[1, rows, :] * phi + waves[2, rows, :]).astype(F32) * TURN_UNIT
                ua = a * a
                ub = b * b
                sin_a = a * poly(ua, SIN_C)
                cos_a = poly(ua, COS_C)
                sin_b = b * poly(ub, SIN_C)
                w = 1.0 - sin_b * sin_b
                sin_w = sin_a * w
                fresh[0, rows, lanes] = (w - sin_a * sin_w).astype(BF16)
                fresh[1, rows, lanes] = (cos_a * sin_w).astype(BF16)
            at = pl.multiple_of(tile * LANES, LANES)
            for c in range(2):
                values = obs_ref[c:c + 1, pl.ds(at, LANES)]
                fresh[c, width:, lanes] = jnp.where(
                    below, jnp.broadcast_to(values, (EXTRA, LANES)), 0.0
                ).astype(BF16)

    def shift():
        window[:, :, taps_n:] = window[:, :, :taps_n]
        window[:, :, :taps_n] = fresh[...]

    window[:, :, :taps_n] = jnp.zeros((2, width + EXTRA, taps_n), BF16)

    @pl.loop(0, 2)
    def _(step):
        design_block(blocks - 1 - step)
        shift()

    if fused:
        pl.semaphore_wait(barrier, len(greeted))
        halo_copy = copy(halo_send, halo, 0, after)

    j = lax.broadcasted_iota(jnp.int32, (taps_n, taps_n), 0)
    i = lax.broadcasted_iota(jnp.int32, (taps_n, taps_n), 1)
    for c in range(2):
        row = jnp.broadcast_to(taps_ref[c:c + 1, :].astype(F32), (8, taps_n))
        base = pltpu.roll(row, 0, 1, stride=1, stride_axis=0)
        for r in range(0, taps_n, 8):
            around = pltpu.roll(base, r, 1) if r else base
            early = i[r:r + 8] < j[r:r + 8]
            table[c, r:r + 8, :] = jnp.where(early, around, 0.0)
            table[c, taps_n + r:taps_n + r + 8, :] = jnp.where(early, 0.0, around)

    first_lane = lax.broadcasted_iota(jnp.int32, (LANES, LANES), 0)
    second_lane = lax.broadcasted_iota(jnp.int32, (LANES, LANES), 1)
    ones = jnp.ones((LANES, LANES), BF16)

    def counted(flags, lanes, rows):
        here = jnp.dot(flags, lanes.astype(BF16), preferred_element_type=F32)
        others = jnp.dot(rows.astype(BF16), flags, preferred_element_type=F32)
        return here + jnp.dot(others.astype(BF16), ones, preferred_element_type=F32)

    first_row = lax.broadcasted_iota(jnp.int32, (own, own), 0)
    second_row = lax.broadcasted_iota(jnp.int32, (own, own), 1)
    lab[0:own] = counted(
        seg_ref[...].astype(F32).astype(BF16), first_lane <= second_lane, second_row < first_row
    )
    if fused:
        halo_copy.wait()
    first_row = lax.broadcasted_iota(jnp.int32, (halo.shape[0], halo.shape[0]), 0)
    second_row = lax.broadcasted_iota(jnp.int32, (halo.shape[0], halo.shape[0]), 1)
    later = (first_row < second_row) & (second_row < 3 * per)
    ahead = counted(halo[...].astype(BF16), first_lane > second_lane, later)
    first = row_index == 0
    lab[own:own + per] = jnp.where(first, -1.0, -ahead[2 * per:3 * per])
    for r in range(per):
        for c in range(2):
            at = (3 + c) * per + r
            obs_ref[c:c + 1, (own + r) * LANES:(own + r + 1) * LANES] = halo[at:at + 1]
    col_ref[own:own + per] = halo[0:per]
    lon_ref[own:own + per] = halo[per:2 * per]
    turned[0:own + per] = lab[...]
    columns = turned[...].T
    for tile in range(own + per):
        lab_col[tile * LANES:(tile + 1) * LANES, :] = spread(columns, tile)

    half_width = width // 2
    half_tiles = half_width // LANES
    gram[...] = jnp.zeros(gram.shape, F32)
    filt[...] = jnp.zeros(filt.shape, BF16)

    def filter_block(block):
        slots = (lax.rem(block + blocks, blocks + 1), block)
        for half in range(per):
            lanes = slice(half * LANES, (half + 1) * LANES)
            out_label = lab[pl.ds(block * per + half, 1), :]
            for part in range(2 * per):
                at = slice(part * LANES, (part + 1) * LANES)
                tile = slots[part // per] * per + part % per
                got = lab_col[pl.ds(pl.multiple_of(tile * LANES, LANES), LANES), :]
                same = got == out_label
                for c in range(2):
                    matrix[c, at, lanes] = jnp.where(same, table[c, at, lanes], 0.0).astype(BF16)
        for c in range(2):
            filt_next[:, c * taps_n:(c + 1) * taps_n] = jnp.dot(
                window[c], matrix[c], preferred_element_type=F32
            ).astype(BF16)

    def gram_half(half):
        from_row = half * half_width
        part = lax.dot_general(
            filt[from_row:, :], filt[from_row:from_row + half_width, :],
            (((1,), (1,)), ((), ())), preferred_element_type=F32,
        )
        for t in range(half_tiles):
            gram[half * half_tiles + t, from_row:, :] += part[:, t * LANES:(t + 1) * LANES]

    @pl.loop(0, blocks - 1)
    def _(step):
        block = blocks - 1 - step
        gram_half(0)
        gram_half(1)
        filter_block(block)
        design_block(lax.rem(block - 2 + blocks + 1, blocks + 1))
        shift()
        filt[...] = filt_next[...]

    gram_half(0)
    gram_half(1)
    filter_block(0)
    filt[...] = filt_next[...]
    copies_a = []
    for half in range(2):
        gram_half(half)
        if half == 1:
            for t in range(half_tiles):
                for q in range(half_tiles):
                    gram[half_tiles + t, q * LANES:(q + 1) * LANES, :] = gram[
                        q, half_width + t * LANES:half_width + (t + 1) * LANES, :].T
        if fused:
            tile_rows = width // n_row
            for t in range(half * half_tiles, (half + 1) * half_tiles):
                for zz in range(n_z):
                    at = pl.multiple_of((2 * zz + 1 - core) * tile_rows, tile_rows)
                    sa[t, zz] = gram[t, pl.ds(at, tile_rows), :].astype(BF16)
            part = pl.ds(half * half_tiles, half_tiles)
            copies_a.append(copy(sa.at[part], ra.at[part], 1 + half, twin))

    eye = lax.broadcasted_iota(jnp.int32, (LANES, LANES), 0) == lax.broadcasted_iota(
        jnp.int32, (LANES, LANES), 1
    )
    small = []
    for t in range(col_tiles):
        small.append(gram[t, width:width + 1, :])
    for t in range(col_tiles):
        square = gram[t, t * LANES:(t + 1) * LANES, :]
        small.append(jnp.sum(jnp.where(eye, square, 0.0), axis=0, keepdims=True))
    if not fused:
        for r, row in enumerate(small):
            small_ref[r:r + 1, :] = row
        return

    for r, row in enumerate(small):
        rs[0, r:r + 1, :] = row
    small_a = copy(rs.at[0], rr.at[0], 3, twin)
    for c in copies_a:
        c.wait()
    for t in range(col_tiles):
        for zz in range(n_z):
            at = pl.multiple_of((2 * zz + core) * tile_rows, tile_rows)
            gram[t, pl.ds(zz * tile_rows, tile_rows), :] = gram[
                t, pl.ds(at, tile_rows), :] + ra[t, zz].astype(F32)

    def held(t, zz):
        return gram[t, pl.ds(pl.multiple_of(zz * tile_rows, tile_rows), tile_rows), :]

    small_a.wait()
    rx[grp_index] = rs[0] + rr[0]
    small_b = [
        copy(rx.at[grp_index], rx.at[grp_index], 3 + k, grp_peers[k - 1]) for k in range(1, n_grp)
    ]
    offsets = [(dg, dz) for dz in (2, 1, 3, 0) for dg in (3, 2, 1, 0) if dg or dz]
    copies_b = []
    for dg, dz in offsets:
        slot = dg * n_z + dz
        there = (lax.rem(grp_index + dg, n_grp), lax.rem(z + dz, n_z))
        sb[slot] = held(*there).astype(BF16)
        copies_b.append(copy(
            sb.at[slot], rb.at[slot], 10 + slot, (there[0], 2 * there[1] + core)
        ))
    for c in small_b:
        c.wait()
    total = rx[0]
    for g in range(1, n_grp):
        total = total + rx[g]
    rz[z] = total
    small_d = [copy(rz.at[z], rz.at[z], 6 + k, z_peers[k - 1]) for k in range(1, n_z)]
    total = held(grp_index, z)
    for (dg, dz), c in zip(offsets, copies_b):
        c.wait()
        total = total + rb[dg * n_z + dz].astype(F32)
    row_at = row_index * tile_rows + lax.broadcasted_iota(jnp.int32, total.shape, 0)
    col_at = grp_index * LANES + lax.broadcasted_iota(jnp.int32, total.shape, 1)
    out_ref[...] = jnp.where(row_at == col_at, 0.0, total * gram_scale)
    for c in small_d:
        c.wait()
    total = rz[0]
    for zz in range(1, n_z):
        total = total + rz[zz]
    right_ref[...] = total[0:col_tiles] * gram_scale
    diag_ref[...] = total[col_tiles:] * row_scale


def on_device(colatitude, longitude, observed, filter_taps, segment_start, harmonic):
    rows_here = colatitude.shape[0]
    taps_n = filter_taps.shape[1]
    width = harmonic.shape[1]
    n_grp = lax.axis_size("grp")
    n_row = lax.axis_size("row")
    blocks = rows_here // taps_n
    per = taps_n // LANES
    tiles = width // LANES
    rows_total = rows_here * n_grp * n_row
    row_scale = 1.0 / rows_total
    gram_scale = 1.0 / math.sqrt(rows_total)
    fused = FUSED and n_grp == 4 and n_row == 8 and width == n_grp * LANES
    split = [a.reshape(rows_here // LANES, LANES) for a in (colatitude, longitude, segment_start)]
    inputs = [split[0], split[1], observed, filter_taps, split[2], harmonic]
    window = rows_here + taps_n
    scratch = [
        pltpu.VMEM((window // LANES, LANES), F32),
        pltpu.VMEM((window // LANES, LANES), F32),
        pltpu.VMEM(observed.shape, observed.dtype),
        pltpu.VMEM(filter_taps.shape, filter_taps.dtype),
        pltpu.VMEM((rows_here // LANES, LANES), segment_start.dtype),
        pltpu.VMEM(harmonic.shape, harmonic.dtype),
        pltpu.SemaphoreType.DMA((6,)),
        pltpu.VMEM((2, window), F32),
        pltpu.VMEM((2, width + EXTRA, taps_n), BF16),
        pltpu.VMEM((2, width + EXTRA, 2 * taps_n), BF16),
        pltpu.VMEM((width + EXTRA, 2 * taps_n), BF16),
        pltpu.VMEM((width + EXTRA, 2 * taps_n), BF16),
        pltpu.VMEM((2, 2 * taps_n, taps_n), F32),
        pltpu.VMEM((2, 2 * taps_n, taps_n), BF16),
        pltpu.VMEM((window, LANES), F32),
        pltpu.VMEM((window // LANES, LANES), F32),
        pltpu.VMEM((3, width, LANES), jnp.int32),
        pltpu.VMEM((LANES, LANES), F32),
    ]
    gram_shape = (tiles, width + EXTRA, LANES)
    small_shapes = (jax.ShapeDtypeStruct((2 * tiles, LANES), F32),)
    halo_shape = (8 * per, LANES)
    if fused:
        tile_rows = width // n_row
        n_z = n_row // 2
        tile = (tile_rows, LANES)
        copies = 10 + n_grp * n_z
        scratch += [
            pltpu.VMEM(gram_shape, F32),
            pltpu.VMEM(halo_shape, F32),
            pltpu.VMEM(halo_shape, F32),
            pltpu.VMEM((tiles, n_z) + tile, BF16),
            pltpu.VMEM((tiles, n_z) + tile, BF16),
            pltpu.VMEM((n_grp * n_z,) + tile, BF16),
            pltpu.VMEM((n_grp * n_z,) + tile, BF16),
            pltpu.VMEM((1, 2 * tiles, LANES), F32),
            pltpu.VMEM((1, 2 * tiles, LANES), F32),
            pltpu.VMEM((n_grp, 2 * tiles, LANES), F32),
            pltpu.VMEM((n_z, 2 * tiles, LANES), F32),
            pltpu.SemaphoreType.DMA((copies,)),
            pltpu.SemaphoreType.DMA((copies,)),
        ]
        main_shape = jax.ShapeDtypeStruct((tile_rows, LANES), F32)
        small_shapes = (jax.ShapeDtypeStruct((tiles, LANES), F32),) * 2
    else:
        last = rows_here // LANES - per
        pieces = [split[0][last:], split[1][last:], split[2][last:].astype(F32)]
        pieces.append(observed[:, rows_here - taps_n:].astype(F32).reshape(2 * per, LANES))
        pieces.append(jnp.zeros((3 * per, LANES), F32))
        pairs = [(k, k + 1) for k in range(n_row - 1)]
        inputs.append(lax.ppermute(jnp.concatenate(pieces), "row", pairs))
        main_shape = jax.ShapeDtypeStruct(gram_shape, F32)
    params = dict(vmem_limit_bytes=64 * 1024 * 1024)
    if fused:
        params.update(collective_id=0, has_side_effects=True)
    main, *small = pl.pallas_call(
        functools.partial(
            local_kernel, fused, n_grp, n_row, blocks, taps_n, width, gram_scale, row_scale
        ),
        out_shape=(main_shape,) + small_shapes,
        in_specs=[pl.BlockSpec(memory_space=pltpu.HBM)] * 6
        + [pl.BlockSpec(memory_space=pltpu.VMEM)] * (len(inputs) - 6),
        out_specs=(pl.BlockSpec(memory_space=pltpu.VMEM),) * (1 + len(small_shapes)),
        scratch_shapes=scratch,
        compiler_params=pltpu.CompilerParams(**params),
        name="normal_equations",
    )(*inputs)
    if fused:
        results = (main,) + tuple(small)
        normal, right_side, diagonal = pl.pallas_call(
            hand_on_kernel,
            out_shape=tuple(jax.ShapeDtypeStruct(r.shape, r.dtype) for r in results),
            in_specs=[pl.BlockSpec(memory_space=pl.ANY)] * 3,
            out_specs=(pl.BlockSpec(memory_space=pl.ANY),) * 3,
            scratch_shapes=[pltpu.SemaphoreType.DMA((3,))],
            compiler_params=pltpu.CompilerParams(vmem_limit_bytes=64 * 1024 * 1024),
            name="hand_on",
        )(*results)
        return (normal, right_side.reshape(width), diagonal.reshape(width))
    small = small[0]
    gram = main[:, :width].transpose(1, 0, 2).reshape(width, width)
    owned = lax.psum_scatter(gram, "row", scatter_dimension=0, tiled=True)
    normal = lax.psum_scatter(owned, "grp", scatter_dimension=1, tiled=True)
    small = lax.psum(small, ("grp", "row"))
    row_at = lax.axis_index("row") * normal.shape[0] + lax.broadcasted_iota(
        jnp.int32, normal.shape, 0
    )
    col_at = lax.axis_index("grp") * normal.shape[1] + lax.broadcasted_iota(
        jnp.int32, normal.shape, 1
    )
    normal = jnp.where(row_at == col_at, 0.0, normal * gram_scale)
    right_side = small[:tiles].reshape(width) * gram_scale
    diagonal = small[tiles:].reshape(width) * row_scale
    return (normal, right_side, diagonal)


def solution(mesh):
    placed = (
        P(("grp", "row")),
        P(("grp", "row")),
        P(None, ("grp", "row")),
        P(),
        P(("grp", "row")),
        P(),
    )
    return jax.shard_map(
        on_device,
        mesh=mesh,
        in_specs=placed,
        out_specs=(P("row", "grp"), P(), P()),
        check_vma=False,
    )
```

```python
import functools
import math

import jax
import jax.numpy as jnp
from jax import lax
from jax.experimental import pallas as pl
from jax.experimental.pallas import tpu as pltpu
from jax.sharding import PartitionSpec as P

F32 = jnp.float32
BF16 = jnp.bfloat16
LANES = 128
EXTRA = 16
CHUNK = 64
SIN_C = (4.442866325378418, -7.307384967803955, 3.594230890274048, -0.7829042077064514)
COS_C = (1.41420316696167, -6.977553367614746, 5.714066982269287, -1.7246402502059937)
TURN_HIGH = 2608.0 / 16384.0
TURN_LOW = 1.0 / (2.0 * math.pi) - TURN_HIGH
TURN_UNIT = 2.0**-32
FUSED = True


def poly(u, coefficients):
    total = coefficients[-1]
    for c in coefficients[-2::-1]:
        total = total * u + c
    return total


def nearest(x):
    return (x + 12582912.0) - 12582912.0


def spread(columns, k):
    return jnp.broadcast_to(columns[:, k:k + 1], (LANES, LANES))


def turns(angle):
    head = nearest(angle * 1024.0) * (1.0 / 1024.0)
    tail = angle - head
    coarse = head * TURN_HIGH
    high = nearest(coarse * 32768.0)
    low = (coarse - high * (1.0 / 32768.0)) + (head * TURN_LOW + tail * (TURN_HIGH + TURN_LOW))
    fine = nearest(low * 2.0**32)
    return high.astype(jnp.int32) * 131072 + fine.astype(jnp.int32)


def hand_on_kernel(*refs):
    count = (len(refs) - 1) // 2
    copies = [
        pltpu.make_async_copy(refs[k], refs[count + k], refs[-1].at[k]) for k in range(count)
    ]
    for c in copies:
        c.start()
    for c in copies:
        c.wait()


def local_kernel(
    fused, n_grp, n_row, blocks, taps_n, width, gram_scale, row_scale,
    col_in, lon_in, obs_in, taps_in, seg_in, har_in, *refs,
):
    if fused:
        (out_ref, right_ref, diag_ref, col_ref, lon_ref, obs_got, taps_ref, seg_ref, har_ref, in_sem,
         obs_ref, fresh, window, filt, filt_next, table, matrix, lab_col, lab, waves, turned, gram,
         halo_send, halo, sa, ra, sb, rb, rs, rr, rx, rz, send_sem, recv_sem) = refs
    else:
        (halo, gram, small_ref, col_ref, lon_ref, obs_got, taps_ref, seg_ref, har_ref, in_sem,
         obs_ref, fresh, window, filt, filt_next, table, matrix, lab_col, lab, waves, turned) = refs
    per = taps_n // LANES
    own = blocks * per
    col_tiles = width // LANES
    row_index = lax.axis_index("row")
    grp_index = lax.axis_index("grp")

    fetched = (
        (har_in, har_ref), (taps_in, taps_ref), (col_in, col_ref.at[0:own]),
        (lon_in, lon_ref.at[0:own]), (seg_in, seg_ref), (obs_in, obs_got),
    )
    fetches = [
        pltpu.make_async_copy(src, dst, in_sem.at[k]) for k, (src, dst) in enumerate(fetched)
    ]
    for fetch in fetches:
        fetch.start()

    if fused:
        core = lax.rem(row_index, 2)
        z = row_index // 2
        n_z = n_row // 2
        twin = (grp_index, row_index + 1 - 2 * core)
        grp_peers = [(lax.rem(grp_index + k, n_grp), row_index) for k in range(1, n_grp)]
        z_peers = [(grp_index, lax.rem(row_index + 2 * k, n_row)) for k in range(1, n_z)]
        after = (grp_index, lax.rem(row_index + 1, n_row))
        before = (grp_index, lax.rem(row_index + n_row - 1, n_row))
        greeted = [twin, after, before] + grp_peers + z_peers
        barrier = pltpu.get_barrier_semaphore()
        for peer in greeted:
            pl.semaphore_signal(barrier, inc=1, device_id=peer, device_id_type=pl.DeviceIdType.MESH)

        def copy(src, dst, number, peer):
            c = pltpu.make_async_remote_copy(
                src_ref=src, dst_ref=dst,
                send_sem=send_sem.at[number], recv_sem=recv_sem.at[number],
                device_id=peer, device_id_type=pl.DeviceIdType.MESH,
            )
            c.start()
            return c

    for fetch in fetches:
        fetch.wait()
    obs_ref[:, 0:own * LANES] = obs_got[...].astype(F32)

    if fused:
        last = own - per
        halo_send[0:per] = col_ref[last:last + per]
        halo_send[per:2 * per] = lon_ref[last:last + per]
        halo_send[2 * per:3 * per] = seg_ref[last:last + per].astype(F32)
        for c in range(2):
            for p in range(per):
                at = (last + p) * LANES
                halo_send[(3 + c) * per + p:(3 + c) * per + p + 1] = obs_ref[
                    c:c + 1, at:at + LANES]
        halo_send[5 * per:] = jnp.zeros((halo_send.shape[0] - 5 * per, LANES), F32)

    degree = har_ref[0:1, :].astype(F32)
    order = har_ref[1:2, :]
    size = jnp.abs(order).astype(F32)
    phase = jnp.where(order >= 0, 0.0, -1.0).astype(F32)
    turned[...] = jnp.zeros((LANES, LANES), F32)
    number = 0
    for values in (degree, size, phase):
        for t in range(col_tiles):
            turned[number:number + 1, :] = values[:, t * LANES:(t + 1) * LANES]
            number += 1
    columns = turned[...].T
    for number in range(3):
        for t in range(col_tiles):
            unit = 1 << 30 if number == 2 else 1
            waves[number, t * LANES:(t + 1) * LANES, :] = (
                spread(columns, number * col_tiles + t).astype(jnp.int32) * unit
            )

    below = lax.broadcasted_iota(jnp.int32, (EXTRA, LANES), 0) == 0

    def design_block(slot):
        for half in range(per):
            tile = slot * per + half
            lanes = slice(half * LANES, (half + 1) * LANES)
            theta = turns(col_ref[pl.ds(tile, 1), :])
            phi = turns(lon_ref[pl.ds(tile, 1), :])
            for chunk in range(width // CHUNK):
                rows = slice(chunk * CHUNK, (chunk + 1) * CHUNK)
                a = (waves[0, rows, :] * theta).astype(F32) * TURN_UNIT
                b = (waves[1, rows, :] * phi + waves[2, rows, :]).astype(F32) * TURN_UNIT
                ua = a * a
                ub = b * b
                sin_a = a * poly(ua, SIN_C)
                cos_a = poly(ua, COS_C)
                sin_b = b * poly(ub, SIN_C)
                w = 1.0 - sin_b * sin_b
                sin_w = sin_a * w
                fresh[0, rows, lanes] = (w - sin_a * sin_w).astype(BF16)
                fresh[1, rows, lanes] = (cos_a * sin_w).astype(BF16)
            at = pl.multiple_of(tile * LANES, LANES)
            for c in range(2):
                values = obs_ref[c:c + 1, pl.ds(at, LANES)]
                fresh[c, width:, lanes] = jnp.where(
                    below, jnp.broadcast_to(values, (EXTRA, LANES)), 0.0
                ).astype(BF16)

    def shift():
        window[:, :, taps_n:] = window[:, :, :taps_n]
        window[:, :, :taps_n] = fresh[...]

    window[:, :, :taps_n] = jnp.zeros((2, width + EXTRA, taps_n), BF16)

    @pl.loop(0, 2)
    def _(step):
        design_block(blocks - 1 - step)
        shift()

    if fused:
        pl.semaphore_wait(barrier, len(greeted))
        halo_copy = copy(halo_send, halo, 0, after)

    j = lax.broadcasted_iota(jnp.int32, (taps_n, taps_n), 0)
    i = lax.broadcasted_iota(jnp.int32, (taps_n, taps_n), 1)
    for c in range(2):
        row = jnp.broadcast_to(taps_ref[c:c + 1, :].astype(F32), (8, taps_n))
        base = pltpu.roll(row, 0, 1, stride=1, stride_axis=0)
        for r in range(0, taps_n, 8):
            around = pltpu.roll(base, r, 1) if r else base
            early = i[r:r + 8] < j[r:r + 8]
            table[c, r:r + 8, :] = jnp.where(early, around, 0.0)
            table[c, taps_n + r:taps_n + r + 8, :] = jnp.where(early, 0.0, around)

    first_lane = lax.broadcasted_iota(jnp.int32, (LANES, LANES), 0)
    second_lane = lax.broadcasted_iota(jnp.int32, (LANES, LANES), 1)
    ones = jnp.ones((LANES, LANES), BF16)

    def counted(flags, lanes, rows):
        here = jnp.dot(flags, lanes.astype(BF16), preferred_element_type=F32)
        others = jnp.dot(rows.astype(BF16), flags, preferred_element_type=F32)
        return here + jnp.dot(others.astype(BF16), ones, preferred_element_type=F32)

    first_row = lax.broadcasted_iota(jnp.int32, (own, own), 0)
    second_row = lax.broadcasted_iota(jnp.int32, (own, own), 1)
    lab[0:own] = counted(
        seg_ref[...].astype(F32).astype(BF16), first_lane <= second_lane, second_row < first_row
    )
    if fused:
        halo_copy.wait()
    first_row = lax.broadcasted_iota(jnp.int32, (halo.shape[0], halo.shape[0]), 0)
    second_row = lax.broadcasted_iota(jnp.int32, (halo.shape[0], halo.shape[0]), 1)
    later = (first_row < second_row) & (second_row < 3 * per)
    ahead = counted(halo[...].astype(BF16), first_lane > second_lane, later)
    first = row_index == 0
    lab[own:own + per] = jnp.where(first, -1.0, -ahead[2 * per:3 * per])
    for r in range(per):
        for c in range(2):
            at = (3 + c) * per + r
            obs_ref[c:c + 1, (own + r) * LANES:(own + r + 1) * LANES] = halo[at:at + 1]
    col_ref[own:own + per] = halo[0:per]
    lon_ref[own:own + per] = halo[per:2 * per]
    turned[0:own + per] = lab[...]
    columns = turned[...].T
    for tile in range(own + per):
        lab_col[tile * LANES:(tile + 1) * LANES, :] = spread(columns, tile)

    half_width = width // 2
    half_tiles = half_width // LANES
    gram[...] = jnp.zeros(gram.shape, F32)
    filt[...] = jnp.zeros(filt.shape, BF16)

    def filter_block(block):
        slots = (lax.rem(block + blocks, blocks + 1), block)
        for half in range(per):
            lanes = slice(half * LANES, (half + 1) * LANES)
            out_label = lab[pl.ds(block * per + half, 1), :]
            for part in range(2 * per):
                at = slice(part * LANES, (part + 1) * LANES)
                tile = slots[part // per] * per + part % per
                got = lab_col[pl.ds(pl.multiple_of(tile * LANES, LANES), LANES), :]
                same = got == out_label
                for c in range(2):
                    matrix[c, at, lanes] = jnp.where(same, table[c, at, lanes], 0.0).astype(BF16)
        for c in range(2):
            filt_next[:, c * taps_n:(c + 1) * taps_n] = jnp.dot(
                window[c], matrix[c], preferred_element_type=F32
            ).astype(BF16)

    def gram_half(half):
        from_row = half * half_width
        part = lax.dot_general(
            filt[from_row:, :], filt[from_row:from_row + half_width, :],
            (((1,), (1,)), ((), ())), preferred_element_type=F32,
        )
        for t in range(half_tiles):
            gram[half * half_tiles + t, from_row:, :] += part[:, t * LANES:(t + 1) * LANES]

    @pl.loop(0, blocks - 1)
    def _(step):
        block = blocks - 1 - step
        gram_half(0)
        gram_half(1)
        filter_block(block)
        design_block(lax.rem(block - 2 + blocks + 1, blocks + 1))
        shift()
        filt[...] = filt_next[...]

    gram_half(0)
    gram_half(1)
    filter_block(0)
    filt[...] = filt_next[...]
    copies_a = []
    for half in range(2):
        gram_half(half)
        if half == 1:
            for t in range(half_tiles):
                for q in range(half_tiles):
                    gram[half_tiles + t, q * LANES:(q + 1) * LANES, :] = gram[
                        q, half_width + t * LANES:half_width + (t + 1) * LANES, :].T
        if fused:
            tile_rows = width // n_row
            for t in range(half * half_tiles, (half + 1) * half_tiles):
                for zz in range(n_z):
                    at = pl.multiple_of((2 * zz + 1 - core) * tile_rows, tile_rows)
                    sa[t, zz] = gram[t, pl.ds(at, tile_rows), :].astype(BF16)
            part = pl.ds(half * half_tiles, half_tiles)
            copies_a.append(copy(sa.at[part], ra.at[part], 1 + half, twin))

    eye = lax.broadcasted_iota(jnp.int32, (LANES, LANES), 0) == lax.broadcasted_iota(
        jnp.int32, (LANES, LANES), 1
    )
    small = []
    for t in range(col_tiles):
        small.append(gram[t, width:width + 1, :])
    for t in range(col_tiles):
        square = gram[t, t * LANES:(t + 1) * LANES, :]
        small.append(jnp.sum(jnp.where(eye, square, 0.0), axis=0, keepdims=True))
    if not fused:
        for r, row in enumerate(small):
            small_ref[r:r + 1, :] = row
        return

    for r, row in enumerate(small):
        rs[0, r:r + 1, :] = row
    small_a = copy(rs.at[0], rr.at[0], 3, twin)
    for c in copies_a:
        c.wait()
    for t in range(col_tiles):
        for zz in range(n_z):
            at = pl.multiple_of((2 * zz + core) * tile_rows, tile_rows)
            gram[t, pl.ds(zz * tile_rows, tile_rows), :] = gram[
                t, pl.ds(at, tile_rows), :] + ra[t, zz].astype(F32)

    def held(t, zz):
        return gram[t, pl.ds(pl.multiple_of(zz * tile_rows, tile_rows), tile_rows), :]

    small_a.wait()
    rx[grp_index] = rs[0] + rr[0]
    small_b = [
        copy(rx.at[grp_index], rx.at[grp_index], 3 + k, grp_peers[k - 1]) for k in range(1, n_grp)
    ]
    order = [2, 1, 3, 0]
    across = {}
    for dz in order:
        for dg in range(1, n_grp):
            slot = dg * n_z + dz
            sb[slot] = held(lax.rem(grp_index + dg, n_grp), lax.rem(z + dz, n_z)).astype(BF16)
            across[slot] = copy(sb.at[slot], rb.at[slot], 10 + slot, grp_peers[dg - 1])

    def arc_sum(dz):
        total = held(grp_index, lax.rem(z + dz, n_z))
        for dg in range(1, n_grp):
            across[dg * n_z + dz].wait()
            total = total + rb[dg * n_z + dz].astype(F32)
        return total

    along = []
    for dz in order[:-1]:
        sb[dz] = arc_sum(dz).astype(BF16)
        along.append(copy(sb.at[dz], rb.at[dz], 10 + dz, z_peers[dz - 1]))
    for c in small_b:
        c.wait()
    total = rx[0]
    for g in range(1, n_grp):
        total = total + rx[g]
    rz[z] = total
    small_d = [copy(rz.at[z], rz.at[z], 6 + k, z_peers[k - 1]) for k in range(1, n_z)]
    total = arc_sum(0)
    for dz, c in zip(order[:-1], along):
        c.wait()
        total = total + rb[dz].astype(F32)
    row_at = row_index * tile_rows + lax.broadcasted_iota(jnp.int32, total.shape, 0)
    col_at = grp_index * LANES + lax.broadcasted_iota(jnp.int32, total.shape, 1)
    out_ref[...] = jnp.where(row_at == col_at, 0.0, total * gram_scale)
    for c in small_d:
        c.wait()
    total = rz[0]
    for zz in range(1, n_z):
        total = total + rz[zz]
    right_ref[...] = total[0:col_tiles] * gram_scale
    diag_ref[...] = total[col_tiles:] * row_scale


def on_device(colatitude, longitude, observed, filter_taps, segment_start, harmonic):
    rows_here = colatitude.shape[0]
    taps_n = filter_taps.shape[1]
    width = harmonic.shape[1]
    n_grp = lax.axis_size("grp")
    n_row = lax.axis_size("row")
    blocks = rows_here // taps_n
    per = taps_n // LANES
    tiles = width // LANES
    rows_total = rows_here * n_grp * n_row
    row_scale = 1.0 / rows_total
    gram_scale = 1.0 / math.sqrt(rows_total)
    fused = FUSED and n_grp == 4 and n_row == 8 and width == n_grp * LANES
    split = [a.reshape(rows_here // LANES, LANES) for a in (colatitude, longitude, segment_start)]
    inputs = [split[0], split[1], observed, filter_taps, split[2], harmonic]
    window = rows_here + taps_n
    scratch = [
        pltpu.VMEM((window // LANES, LANES), F32),
        pltpu.VMEM((window // LANES, LANES), F32),
        pltpu.VMEM(observed.shape, observed.dtype),
        pltpu.VMEM(filter_taps.shape, filter_taps.dtype),
        pltpu.VMEM((rows_here // LANES, LANES), segment_start.dtype),
        pltpu.VMEM(harmonic.shape, harmonic.dtype),
        pltpu.SemaphoreType.DMA((6,)),
        pltpu.VMEM((2, window), F32),
        pltpu.VMEM((2, width + EXTRA, taps_n), BF16),
        pltpu.VMEM((2, width + EXTRA, 2 * taps_n), BF16),
        pltpu.VMEM((width + EXTRA, 2 * taps_n), BF16),
        pltpu.VMEM((width + EXTRA, 2 * taps_n), BF16),
        pltpu.VMEM((2, 2 * taps_n, taps_n), F32),
        pltpu.VMEM((2, 2 * taps_n, taps_n), BF16),
        pltpu.VMEM((window, LANES), F32),
        pltpu.VMEM((window // LANES, LANES), F32),
        pltpu.VMEM((3, width, LANES), jnp.int32),
        pltpu.VMEM((LANES, LANES), F32),
    ]
    gram_shape = (tiles, width + EXTRA, LANES)
    small_shapes = (jax.ShapeDtypeStruct((2 * tiles, LANES), F32),)
    halo_shape = (8 * per, LANES)
    if fused:
        tile_rows = width // n_row
        n_z = n_row // 2
        tile = (tile_rows, LANES)
        copies = 10 + n_grp * n_z
        scratch += [
            pltpu.VMEM(gram_shape, F32),
            pltpu.VMEM(halo_shape, F32),
            pltpu.VMEM(halo_shape, F32),
            pltpu.VMEM((tiles, n_z) + tile, BF16),
            pltpu.VMEM((tiles, n_z) + tile, BF16),
            pltpu.VMEM((n_grp * n_z,) + tile, BF16),
            pltpu.VMEM((n_grp * n_z,) + tile, BF16),
            pltpu.VMEM((1, 2 * tiles, LANES), F32),
            pltpu.VMEM((1, 2 * tiles, LANES), F32),
            pltpu.VMEM((n_grp, 2 * tiles, LANES), F32),
            pltpu.VMEM((n_z, 2 * tiles, LANES), F32),
            pltpu.SemaphoreType.DMA((copies,)),
            pltpu.SemaphoreType.DMA((copies,)),
        ]
        main_shape = jax.ShapeDtypeStruct((tile_rows, LANES), F32)
        small_shapes = (jax.ShapeDtypeStruct((tiles, LANES), F32),) * 2
    else:
        last = rows_here // LANES - per
        pieces = [split[0][last:], split[1][last:], split[2][last:].astype(F32)]
        pieces.append(observed[:, rows_here - taps_n:].astype(F32).reshape(2 * per, LANES))
        pieces.append(jnp.zeros((3 * per, LANES), F32))
        pairs = [(k, k + 1) for k in range(n_row - 1)]
        inputs.append(lax.ppermute(jnp.concatenate(pieces), "row", pairs))
        main_shape = jax.ShapeDtypeStruct(gram_shape, F32)
    params = dict(vmem_limit_bytes=64 * 1024 * 1024)
    if fused:
        params.update(collective_id=0, has_side_effects=True)
    main, *small = pl.pallas_call(
        functools.partial(
            local_kernel, fused, n_grp, n_row, blocks, taps_n, width, gram_scale, row_scale
        ),
        out_shape=(main_shape,) + small_shapes,
        in_specs=[pl.BlockSpec(memory_space=pltpu.HBM)] * 6
        + [pl.BlockSpec(memory_space=pltpu.VMEM)] * (len(inputs) - 6),
        out_specs=(pl.BlockSpec(memory_space=pltpu.VMEM),) * (1 + len(small_shapes)),
        scratch_shapes=scratch,
        compiler_params=pltpu.CompilerParams(**params),
        name="normal_equations",
    )(*inputs)
    if fused:
        results = (main,) + tuple(small)
        normal, right_side, diagonal = pl.pallas_call(
            hand_on_kernel,
            out_shape=tuple(jax.ShapeDtypeStruct(r.shape, r.dtype) for r in results),
            in_specs=[pl.BlockSpec(memory_space=pl.ANY)] * 3,
            out_specs=(pl.BlockSpec(memory_space=pl.ANY),) * 3,
            scratch_shapes=[pltpu.SemaphoreType.DMA((3,))],
            compiler_params=pltpu.CompilerParams(vmem_limit_bytes=64 * 1024 * 1024),
            name="hand_on",
        )(*results)
        return (normal, right_side.reshape(width), diagonal.reshape(width))
    small = small[0]
    gram = main[:, :width].transpose(1, 0, 2).reshape(width, width)
    owned = lax.psum_scatter(gram, "row", scatter_dimension=0, tiled=True)
    normal = lax.psum_scatter(owned, "grp", scatter_dimension=1, tiled=True)
    small = lax.psum(small, ("grp", "row"))
    row_at = lax.axis_index("row") * normal.shape[0] + lax.broadcasted_iota(
        jnp.int32, normal.shape, 0
    )
    col_at = lax.axis_index("grp") * normal.shape[1] + lax.broadcasted_iota(
        jnp.int32, normal.shape, 1
    )
    normal = jnp.where(row_at == col_at, 0.0, normal * gram_scale)
    right_side = small[:tiles].reshape(width) * gram_scale
    diagonal = small[tiles:].reshape(width) * row_scale
    return (normal, right_side, diagonal)


def solution(mesh):
    placed = (
        P(("grp", "row")),
        P(("grp", "row")),
        P(None, ("grp", "row")),
        P(),
        P(("grp", "row")),
        P(),
    )
    return jax.shard_map(
        on_device,
        mesh=mesh,
        in_specs=placed,
        out_specs=(P("row", "grp"), P(), P()),
        check_vma=False,
    )
```
